256 devices in a mesh: lm: 64 (over z, y, core), phi: 4 (over x).
Axes of the slice: x: 4, y: 4, z: 8, core: 2. Of those that a mesh axis runs over, the one named last changes fastest.
Arguments:
- spectrum: bfloat16 [1024, 64, 1024], P('phi', 'lm'), may hold values from -6 to 6
- legendre: bfloat16 [1024, 64, 1536], P(None, 'lm', 'phi'), may hold values from -0.1875 to 0.1875
- orders: int32 [64], replicated, may hold values from 0 to 1023, as said below
- quadrature: float32 [1536], P('phi'), may hold values from 0.2 to 1.8
- radius: float32 [256], replicated, may hold values from 0.35 to 1
- radial: float32 [2, 256, 256], replicated, as said below
Outputs:
- spectrum_new: bfloat16 [1024, 64, 1024], P('phi', 'lm')
The draws below stay inside these ranges and needn't reach their ends.
Inputs may be any that keep to these rules, and one draw needn't show every extreme that they name: The 64 orders are distinct and ascend with the index: index j of lm holds the (j+1)-th smallest order. Order 0 and order 1023 are always carried. `radial`: each field's matrix is its diagonal plus independent off-diagonal entries; the diagonal dominates.
All inputs are finite; a program needn't handle non-finite values.
Results may differ from the reference program's by a relative error of at most 0.014.
Values may be sent and summed in bfloat16 or wider, within the bound.
No kernel may reach another device: no remote copies, remote signals or barrier semaphores. Data moves between devices by JAX's collectives and lax.ppermute only.
A program may use at most 64 MiB of HBM per device.

```python
import math
import jax
import jax.numpy as jnp
from jax import lax

LMAX = 1023
NL = 1024
NLAT = 1536
NPHI = 3072
M_DEV = 1
M = 64
NR = 256
N_PHI = 4


def draw_orders(key, part):
    key = jax.random.fold_in(key, 11)
    groups = M // M_DEV
    inner = jax.random.permutation(key, LMAX - 1).astype(jnp.int32) + 1
    picked = jnp.concatenate([jnp.zeros((1,), jnp.int32), inner[:M - 2], jnp.full((1,), LMAX, jnp.int32)])
    ordered = jnp.sort(picked)
    flat = jnp.arange(M, dtype=jnp.int32)
    device = flat // M_DEV
    sweep = flat % M_DEV
    position = jnp.where(sweep % 2 == 0, device, groups - 1 - device)
    return ordered[sweep * groups + position].astype(jnp.int32)


def draw_radial(key, part):
    key = jax.random.fold_in(key, 5)
    first, second = jax.random.split(key)
    diagonal = jax.random.uniform(first, (2, NR), jnp.float32, 0.6, 1.0)
    scatter = jax.random.normal(second, (2, NR, NR), jnp.float32) * jnp.float32(0.25 * NR ** (-0.5))
    index = jnp.arange(NR, dtype=jnp.int32)
    identity = (index[:, None] == index[None, :]).astype(jnp.float32)
    return (scatter + identity[None, :, :] * diagonal[:, :, None]).astype(jnp.float32)


def block_levels(own_key, dims, cuts, smallest, top_value):
    level = 1.0
    for dim, parts in cuts:
        steps = jax.random.uniform(jax.random.fold_in(jax.random.fold_in(own_key, 6), dim), (parts,), jnp.float32, smallest / len(cuts), top_value / len(cuts))
        level = level * jnp.repeat(jnp.exp(steps), dims[dim] // parts).reshape((-1,) + (1,) * (len(dims) - 1 - dim))
    return level


def noise(own_key, shape, width, reach, cuts=(), kind=jnp.bfloat16):
    drawn = jax.random.normal(own_key, shape, jnp.float32) * width
    if len(cuts) > 0:
        drawn = block_levels(own_key, shape, cuts, -0.22, 0.18) * drawn
    return jnp.clip(drawn, min=-reach, max=reach).astype(kind)


def setup_inputs(seed: int = 0) -> dict:
    streams_of = jax.random.split(jax.random.key(seed), 7)
    return {
        "spectrum": noise(streams_of[0], (NL, M, 4 * NR), 1.0, 6.0, ((0, 4), (1, 64))),
        "legendre": noise(streams_of[1], (NL, M, NLAT), NL ** -0.5, 0.1875, ((1, 64), (2, 4))),
        "orders": draw_orders(jax.random.fold_in(streams_of[6], 71), 0),
        "quadrature": jnp.clip(0.2 + 1.5999999 * jax.random.uniform(streams_of[3], (NLAT,), jnp.float32) ** block_levels(streams_of[3], (NLAT,), ((0, 4),), -0.2, 0.2), 0.2, 1.8),
        "radius": jnp.clip(jnp.exp(jax.random.uniform(streams_of[4], (NR,), jnp.float32, math.log(0.35), math.log(1.0))), 0.35, 1.0),
        "radial": draw_radial(jax.random.fold_in(streams_of[6], 71), 0),
    }


time_step = 0.5
rotation = 2.0

def trig_tables(orders):
    order_total = orders.shape[0]
    steps = orders[:, None] * jnp.arange(NPHI, dtype=jnp.int32)[None, :] % NPHI
    angle = steps.astype(jnp.float32) * jnp.float32(2.0 * math.pi / NPHI)
    weight = jnp.where(orders == 0, 1.0, 2.0).astype(jnp.float32)[:, None] / jnp.float32(math.sqrt(order_total))
    synth_cos = (weight * jnp.cos(angle)).astype(jnp.bfloat16)
    synth_sin = (weight * jnp.sin(angle)).astype(jnp.bfloat16)
    plain_cos = jnp.cos(angle).astype(jnp.bfloat16)
    plain_sin = jnp.sin(angle).astype(jnp.bfloat16)
    return (synth_cos, synth_sin, plain_cos, plain_sin)

def reference(spectrum, legendre, orders, quadrature, radius, radial):
    viscosity = 1.0 / (LMAX * (LMAX + 1.0))
    degrees = jnp.arange(NL, dtype=jnp.int32)
    live = degrees[:, None] >= orders[None, :]
    blocks = M // M_DEV
    columns = 4 * NR

    def table_block(index):
        start = (index * M_DEV).astype(jnp.int32)
        rows = lax.dynamic_slice_in_dim(legendre, start, M_DEV, 1)
        mask = lax.dynamic_slice_in_dim(live, start, M_DEV, 1)
        return (jnp.where(mask[:, :, None], rows, jnp.zeros((), jnp.bfloat16)).astype(jnp.float32), start)

    def synth_block(index):
        table, start = table_block(index)
        coeffs = lax.dynamic_slice_in_dim(spectrum, start, M_DEV, 1).astype(jnp.float32)
        return jnp.einsum('lmt,lmk->kmt', table, coeffs).astype(jnp.bfloat16)
    latitude = lax.map(synth_block, jnp.arange(blocks, dtype=jnp.int32))
    latitude = jnp.moveaxis(latitude, 0, 1).reshape(columns, M, NLAT)
    synth_cos, synth_sin, plain_cos, plain_sin = trig_tables(orders)
    synth_cos = synth_cos.astype(jnp.float32)
    synth_sin = synth_sin.astype(jnp.float32)
    plain_cos = plain_cos.astype(jnp.float32)
    plain_sin = plain_sin.astype(jnp.float32)
    scale_back = jnp.float32(math.sqrt(M) / NPHI)

    def shell_work(shell):
        block = lax.dynamic_slice_in_dim(latitude, (shell * 4).astype(jnp.int32), 4, 0).astype(jnp.float32)
        fields = []
        for field in range(2):
            real_part = block[2 * field]
            imag_part = block[2 * field + 1]
            fields.append(jnp.einsum('it,ip->tp', real_part, synth_cos) - jnp.einsum('it,ip->tp', imag_part, synth_sin))
        first = (fields[0] * fields[1]).astype(jnp.bfloat16).astype(jnp.float32)
        second = (fields[0] * fields[0] - fields[1] * fields[1]).astype(jnp.bfloat16).astype(jnp.float32)
        pieces = []
        for product in (first, second):
            pieces.append((jnp.einsum('tp,ip->it', product, plain_cos) * scale_back).astype(jnp.bfloat16))
            pieces.append((-jnp.einsum('tp,ip->it', product, plain_sin) * scale_back).astype(jnp.bfloat16))
        return jnp.stack(pieces, 0)
    spectral = lax.map(shell_work, jnp.arange(NR, dtype=jnp.int32)).reshape(columns, M, NLAT)
    weighted = (spectral.astype(jnp.float32) * quadrature[None, None, :]).astype(jnp.bfloat16)
    ranges = NLAT // N_PHI

    def analysis_block(index):
        table, start = table_block(index)
        values = lax.dynamic_slice_in_dim(weighted, start, M_DEV, 1).astype(jnp.float32)
        table = table.reshape(NL, M_DEV, N_PHI, ranges)
        values = values.reshape(columns, M_DEV, N_PHI, ranges)
        partial_sums = jnp.einsum('lmqt,kmqt->qlmk', table, values).astype(jnp.bfloat16)
        return lax.optimization_barrier(jnp.sum(partial_sums.astype(jnp.float32), axis=0))
    nonlinear = lax.map(analysis_block, jnp.arange(blocks, dtype=jnp.int32))
    nonlinear = jnp.moveaxis(nonlinear, 0, 1).reshape(NL, M, columns)
    base = spectrum.astype(jnp.float32).reshape(NL, M, NR, 2, 2)
    terms = nonlinear.reshape(NL, M, NR, 2, 2)
    degree_float = degrees.astype(jnp.float32)
    factor = rotation * orders.astype(jnp.float32)[None, :] / (degree_float[:, None] + 1.0)
    other = base[:, :, :, ::-1, :]
    spin = jnp.stack([-other[..., 1], other[..., 0]], -1) * factor[:, :, None, None, None]
    stepped = base + time_step * (terms + spin)
    implicit = jnp.einsum('frs,lisfc->lirfc', radial, stepped, precision=lax.Precision.HIGHEST)
    damping = 1.0 / (1.0 + time_step * viscosity * degree_float[:, None] * (degree_float[:, None] + 1.0) / (radius[None, :] * radius[None, :]))
    result = implicit * damping[:, None, :, None, None]
    result = jnp.where(live[:, :, None, None, None], result, jnp.float32(0.0))
    return result.reshape(NL, M, columns).astype(jnp.bfloat16)
```

```python
import functools
import math

import jax
import jax.numpy as jnp
from jax import lax
from jax.experimental import pallas as pl
from jax.experimental.pallas import tpu as pltpu
from jax.sharding import PartitionSpec as P

LMAX = 1023
NPHI = 3072
LANES = 128
BLOCK = 256

time_step = 0.5
rotation = 2.0

bf16 = jnp.bfloat16
f32 = jnp.float32


def grid_kernel(
    x_ref, perm_ref, back_ref, synth_ref, plain_ref, scale_ref, quad_ref, y_ref, a_ref, acc_ref, *, step
):
    blocks = x_ref.shape[0] // BLOCK
    rows = x_ref.shape[1]
    fields = acc_ref.shape[0] // rows
    width = BLOCK // fields
    turned = [
        jnp.dot(perm_ref[...], x_ref[pl.ds(BLOCK * b, BLOCK), :], preferred_element_type=f32)
        for b in range(blocks)
    ]
    for j in range(fields):
        part = jnp.concatenate([turned[b][width * j : width * (j + 1)] for b in range(blocks)], 0)
        a_ref[pl.ds(rows * j, rows), :] = part.T.astype(bf16)
    acc_ref[...] = jnp.zeros_like(acc_ref)

    def body(i, carry):
        start = pl.multiple_of(i * step, step)
        synth = synth_ref[:, pl.ds(start, step)]
        plain = plain_ref[pl.ds(start, step), :]
        for s in range(fields // 2):
            one = pl.ds(2 * rows * s, rows)
            two = pl.ds(2 * rows * s + rows, rows)
            pol = jnp.dot(a_ref[one, :], synth, preferred_element_type=f32)
            tor = jnp.dot(a_ref[two, :], synth, preferred_element_type=f32)
            first = (pol * tor).astype(bf16)
            second = (pol * pol - tor * tor).astype(bf16)
            acc_ref[one, :] += jnp.dot(first, plain, preferred_element_type=f32)
            acc_ref[two, :] += jnp.dot(second, plain, preferred_element_type=f32)
        return carry

    lax.fori_loop(0, NPHI // step, body, 0)
    done = []
    for j in range(fields):
        spectral = (acc_ref[pl.ds(rows * j, rows), :] * scale_ref[...]).astype(bf16).astype(f32)
        done.append((spectral * quad_ref[...]).T.astype(bf16))
    for b in range(blocks):
        part = jnp.concatenate([done[j][width * b : width * (b + 1)] for j in range(fields)], 0)
        y_ref[pl.ds(BLOCK * b, BLOCK), :] = jnp.dot(
            back_ref[...], part, preferred_element_type=f32
        ).astype(bf16)


def grid_call(x, perm, back, synth, plain, scale, quad, fields):
    rows = x.shape[1]
    vmem = pl.BlockSpec(memory_space=pltpu.VMEM)
    return pl.pallas_call(
        functools.partial(grid_kernel, step=768),
        out_shape=jax.ShapeDtypeStruct(x.shape, bf16),
        in_specs=[vmem] * 7,
        out_specs=vmem,
        scratch_shapes=[
            pltpu.VMEM((fields * rows, LANES), bf16),
            pltpu.VMEM((fields * rows, LANES), f32),
        ],
        compiler_params=pltpu.CompilerParams(vmem_limit_bytes=40 * 2**20),
        name="grid",
    )(x, perm, back, synth, plain, scale, quad)


def permutation():
    row = jnp.arange(BLOCK, dtype=jnp.int32)[:, None]
    column = jnp.arange(BLOCK, dtype=jnp.int32)[None, :]
    perm = column == (row % 16) * 16 + 2 * (row // 32) + (row // 16) % 2
    return perm.astype(bf16), perm.T.astype(bf16)


def wave(order, point, turn):
    whole = order * point
    quarter = jnp.round(whole * f32(4.0 / NPHI))
    angle = (whole - quarter * f32(NPHI / 4)) * f32(2.0 * math.pi / NPHI)
    square = angle * angle
    sine = angle * (1.0 + square * (-1 / 6 + square * (1 / 120 + square * (-1 / 5040))))
    cosine = 1.0 + square * (-0.5 + square * (1 / 24 + square * (-1 / 720 + square * (1 / 40320))))
    turns = quarter.astype(jnp.int32) + turn
    value = jnp.where(turns & 1 == 1, cosine, sine)
    return jnp.where(turns & 2 == 2, -value, value)


def trig_tables(orders):
    order_total = orders.shape[0]
    index = jnp.arange(2 * order_total, dtype=jnp.int32)
    part = (index // 16) % 2
    grouped = jnp.broadcast_to(orders.reshape(-1, 1, 16), (order_total // 16, 2, 16)).reshape(-1)
    order = grouped.astype(f32)
    point = jnp.arange(NPHI, dtype=jnp.int32).astype(f32)
    weight = jnp.where(grouped == 0, 1.0, 2.0).astype(f32) / f32(math.sqrt(order_total))
    weight = jnp.where(part == 0, weight, -weight)
    synth = wave(order[:, None], point[None, :], 1 - part[:, None]) * weight[:, None]
    plain = wave(order[None, :], point[:, None], 1 - part[None, :])
    scale = f32(math.sqrt(order_total) / NPHI)
    scale = jnp.where(part == 0, scale, -scale)[None, :]
    return synth.astype(bf16), plain.astype(bf16), scale


def radial_tables(radial):
    shells = radial.shape[1]
    columns = 4 * shells
    b = jnp.arange(columns, dtype=jnp.int32)
    r = jnp.arange(shells, dtype=jnp.int32)
    spread = [
        ((b[None, :] // 4 == r[:, None]) & ((b[None, :] // 2) % 2 == f)).astype(bf16) for f in range(2)
    ]
    grow = (b[:, None] // 4 == r[None, :]).astype(bf16)
    tables = []
    high = radial.astype(bf16)
    low = (radial - high.astype(f32)).astype(bf16)
    for term in (high, low):
        wide = sum(
            jnp.einsum("rs,rb->sb", term[f], spread[f], preferred_element_type=f32) for f in range(2)
        ).astype(bf16)
        tall = jnp.dot(grow, wide, preferred_element_type=f32)
        same = b[:, None] % 4 == b[None, :] % 4
        cross = 3 - b[:, None] % 4 == b[None, :] % 4
        sign = jnp.where(b % 2 == 0, 1.0, -1.0).astype(f32)[:, None]
        tables.append(jnp.where(same, tall, 0.0).astype(bf16))
        tables.append(jnp.where(cross, tall * sign, 0.0).astype(bf16))
    return tables


def on_device(spectrum, legendre, orders, quadrature, radius, radial):
    viscosity = 1.0 / (LMAX * (LMAX + 1.0))
    degree_dev, _, columns = spectrum.shape
    ring = lax.axis_size("phi")
    group = lax.axis_size("lm")
    shells = columns // 4
    here = lax.axis_index("phi")
    mine = lax.dynamic_slice_in_dim(orders, lax.axis_index("lm"), 1)
    half = degree_dev // 2
    right = [(i, (i + 1) % ring) for i in range(ring)]
    left = [(i, (i - 1) % ring) for i in range(ring)]

    def go(x, way):
        return lax.ppermute(x, "phi", way)

    base = spectrum.reshape(degree_dev, columns)
    top, bottom = base[:half], base[half:]
    below_top = go(top, right)
    above_bottom = go(bottom, left)
    below_bottom = go(bottom, right)
    above_top = go(top, left)
    far_top = go(below_top, right)
    far_bottom = go(above_bottom, left)

    degrees = jnp.arange(legendre.shape[0], dtype=jnp.int32)
    table = jnp.where((degrees >= mine[0])[:, None], legendre[:, 0, :], jnp.zeros((), bf16))

    def rows_of(shift, first, count):
        start = ((here + shift) % ring) * degree_dev + first
        return lax.dynamic_slice_in_dim(table, start, count, 0)

    def synth(piece, rows):
        return jnp.einsum("lk,lt->kt", piece, rows, preferred_element_type=f32)

    near = synth(base, rows_of(0, 0, degree_dev))
    near = near + synth(below_top, rows_of(-1, 0, half)) + synth(above_bottom, rows_of(1, half, half))
    near = near + synth(below_bottom, rows_of(-1, half, half)) + synth(above_top, rows_of(1, 0, half))
    far = synth(far_top, rows_of(2, 0, half)) + synth(far_bottom, rows_of(2, half, half))
    latitude = (near + far).astype(bf16)

    rows = latitude.shape[1]
    per = columns // group
    spread = lax.all_to_all(
        latitude.reshape(group, per, rows), "lm", split_axis=0, concat_axis=0, tiled=True
    )
    perm, back = permutation()
    plain_tables = trig_tables(orders)
    weighted = grid_call(
        spread.reshape(columns, rows), perm, back, *plain_tables, quadrature[:, None], per // 2
    )
    weighted = lax.all_to_all(
        weighted.reshape(group, per, rows), "lm", split_axis=0, concat_axis=0, tiled=True
    ).reshape(columns, rows)

    def project(shift):
        return jnp.einsum(
            "lt,kt->lk", rows_of(shift, 0, degree_dev), weighted, preferred_element_type=f32
        )

    far_part = project(2).astype(bf16)
    from_left = go(far_part[:half], right)
    from_right = go(far_part[half:], left)
    above = project(1)
    below = project(-1)
    sum_bottom = go(above[half:].astype(bf16), right)
    sum_top_left = go(below[:half].astype(bf16), left)
    own = project(0)
    sum_top = go((above[:half] + from_left.astype(f32)).astype(bf16), right)
    sum_bottom_left = go((below[half:] + from_right.astype(f32)).astype(bf16), left)
    other = jnp.concatenate(
        [
            sum_top.astype(f32) + sum_top_left.astype(f32),
            sum_bottom.astype(f32) + sum_bottom_left.astype(f32),
        ],
        0,
    )
    nonlinear = (own + other).astype(bf16)

    local = here * degree_dev + jnp.arange(degree_dev, dtype=jnp.int32)
    degree = local.astype(f32)[:, None]
    straight, turned, straight_low, turned_low = radial_tables(radial)

    def mul(x, y):
        return jnp.dot(x, y, preferred_element_type=f32)

    factor = rotation * mine.astype(f32)[:, None] / (degree + 1.0)
    linear = mul(base, straight) + mul(base, straight_low)
    linear = linear + time_step * factor * (mul(base, turned) + mul(base, turned_low))
    wide_radius = jnp.broadcast_to(radius[:, None], (shells, 4)).reshape(1, columns)
    damping = 1.0 / (
        1.0 + time_step * viscosity * degree * (degree + 1.0) / (wide_radius * wide_radius)
    )
    damping = jnp.where((local >= mine[0])[:, None], damping, 0.0)
    result = (linear + time_step * mul(nonlinear, straight)) * damping
    return result.astype(bf16).reshape(degree_dev, 1, columns)


def solution(mesh):
    return jax.shard_map(
        on_device,
        mesh=mesh,
        in_specs=(P("phi", "lm", None), P(None, "lm", "phi"), P(), P("phi"), P(), P()),
        out_specs=P("phi", "lm", None),
        check_vma=False,
    )
```

```python
import functools
import math

import jax
import jax.numpy as jnp
from jax import lax
from jax.experimental import pallas as pl
from jax.experimental.pallas import tpu as pltpu
from jax.sharding import PartitionSpec as P

LMAX = 1023
NPHI = 3072
LANES = 128
BLOCK = 256

time_step = 0.5
rotation = 2.0

bf16 = jnp.bfloat16
f32 = jnp.float32


def iota(shape, axis):
    return lax.broadcasted_iota(jnp.int32, shape, axis)


def permutation():
    row, column = iota((BLOCK, BLOCK), 0), iota((BLOCK, BLOCK), 1)
    perm = column == (row & 15) * 16 + 2 * (row >> 5) + ((row >> 4) & 1)
    back = row == (column & 15) * 16 + 2 * (column >> 5) + ((column >> 4) & 1)
    return as_ones(perm), as_ones(back)


def as_ones(mask):
    return jnp.where(mask, 1.0, 0.0).astype(bf16)


def grid_kernel(
    x_hbm, synth_hbm, plain_hbm, quad_hbm, y_hbm,
    x_ref, synth_ref, plain_ref, quad_ref, y_ref, a_ref, product_ref, sems, *, step, orders
):
    arrivals = [
        pltpu.make_async_copy(src, dst, sems.at[n])
        for n, (src, dst) in enumerate(
            [(x_hbm, x_ref), (synth_hbm, synth_ref), (plain_hbm, plain_ref), (quad_hbm, quad_ref)]
        )
    ]
    for arrival in arrivals:
        arrival.start()
    blocks = x_ref.shape[0] // BLOCK
    rows = x_ref.shape[1]
    tiles = [(s, t) for s in range(a_ref.shape[0] // (rows // LANES)) for t in range(rows // LANES)]
    fields = 2 * len(tiles) // (rows // LANES)
    width = BLOCK // fields
    perm, back = permutation()
    arrivals[0].wait()
    turned = [
        jnp.dot(perm, x_ref[pl.ds(BLOCK * b, BLOCK), :], preferred_element_type=f32).astype(bf16)
        for b in range(blocks)
    ]
    for j, (s, t) in enumerate(tiles):
        for f in range(2):
            first = width * (2 * s + f)
            for b in range(blocks):
                a_ref[j, pl.ds(width * b, width), pl.ds(LANES * f, LANES)] = turned[b][
                    first : first + width, LANES * t : LANES * (t + 1)
                ]
    for arrival in arrivals[1:]:
        arrival.wait()
    scale = f32(math.sqrt(orders) / NPHI)
    signed = jnp.where(iota((LANES, 1), 0) & 16 == 0, scale, -scale)
    done = []
    for j, (s, t) in enumerate(tiles):
        slot = j % 2
        for n in range(NPHI // step):
            points = pl.ds(step * n, step)
            grid = jnp.dot(synth_ref[points, :], a_ref[j], preferred_element_type=f32)
            pol, tor = grid[:, :LANES], grid[:, LANES:]
            product_ref[slot, points, pl.ds(0, LANES)] = (pol * tor).astype(bf16)
            product_ref[slot, points, pl.ds(LANES, LANES)] = (pol * pol - tor * tor).astype(bf16)
        part = jnp.dot(plain_ref[...], product_ref[slot], preferred_element_type=f32)
        spectral = (part * signed).astype(bf16).astype(f32)
        quad = quad_ref[:, LANES * t : LANES * (t + 1)]
        done.append((spectral * jnp.concatenate([quad, quad], 1)).astype(bf16))
    departures = []
    for b in range(blocks):
        strips = []
        for t in range(rows // LANES):
            strips.append(
                jnp.concatenate(
                    [
                        done[j][width * b : width * (b + 1), LANES * f : LANES * (f + 1)]
                        for j, (s, at) in enumerate(tiles) if at == t
                        for f in range(2)
                    ],
                    0,
                )
            )
        block = pl.ds(BLOCK * b, BLOCK)
        part = jnp.concatenate(strips, 1)
        y_ref[block, :] = jnp.dot(back, part, preferred_element_type=f32).astype(bf16)
        departure = pltpu.make_async_copy(y_ref.at[block], y_hbm.at[block], sems.at[4 + b])
        departure.start()
        departures.append(departure)
    for departure in departures:
        departure.wait()


def grid_call(x, synth, plain, quad, fields, orders):
    rows = x.shape[1]
    anywhere = pl.BlockSpec(memory_space=pltpu.HBM)
    return pl.pallas_call(
        functools.partial(grid_kernel, step=512, orders=orders),
        out_shape=jax.ShapeDtypeStruct(x.shape, bf16),
        in_specs=[anywhere] * 4,
        out_specs=anywhere,
        scratch_shapes=[
            pltpu.VMEM(x.shape, bf16),
            pltpu.VMEM(synth.shape, bf16),
            pltpu.VMEM(plain.shape, bf16),
            pltpu.VMEM(quad.shape, f32),
            pltpu.VMEM(x.shape, bf16),
            pltpu.VMEM((fields // 2 * rows // LANES, LANES, 2 * LANES), bf16),
            pltpu.VMEM((2, NPHI, 2 * LANES), bf16),
            pltpu.SemaphoreType.DMA((4 + x.shape[0] // BLOCK,)),
        ],
        compiler_params=pltpu.CompilerParams(vmem_limit_bytes=58 * 2**20),
        name="grid",
    )(x, synth, plain, quad)


def wave(order, point, turn):
    product = order * point
    quarter = jnp.floor(product * f32(4.0 / NPHI) + f32(0.5))
    angle = (product - quarter * f32(NPHI / 4)) * f32(2.0 * math.pi / NPHI)
    square = angle * angle
    sine = angle * (1.0 + square * (-1 / 6 + square * (1 / 120 + square * (-1 / 5040))))
    cosine = 1.0 + square * (-0.5 + square * (1 / 24 + square * (-1 / 720 + square * (1 / 40320))))
    turns = quarter.astype(jnp.int32) + turn
    value = jnp.where(turns & 1 == 1, cosine, sine)
    return jnp.where(turns & 2 == 2, -value, value)


def trig_tables(orders, synth_ref, plain_ref, step=512):
    total = orders.shape[1]
    values = orders.astype(f32)
    picked = iota((2 * total, total), 0)
    picked = (picked >> 5) * 16 + (picked & 15) == iota((2 * total, total), 1)
    down = jnp.sum(jnp.where(picked, values, 0.0), axis=1, keepdims=True)
    diagonal = iota((total, total), 0) == iota((total, total), 1)
    column = jnp.sum(jnp.where(diagonal, values, 0.0), axis=1, keepdims=True)
    picked = iota((total, 2 * total), 1)
    picked = (picked >> 5) * 16 + (picked & 15) == iota((total, 2 * total), 0)
    across = jnp.sum(jnp.where(picked, column, 0.0), axis=0, keepdims=True)
    part = (iota((2 * total, 1), 0) >> 4) & 1
    part_across = (iota((1, 2 * total), 1) >> 4) & 1
    weight = jnp.where(across == 0, 1.0, 2.0) / f32(math.sqrt(total))
    weight = jnp.where(part_across == 0, weight, -weight)

    def body(i, carry):
        start = pl.multiple_of(i * step, step)
        point = (start + iota((step, 1), 0)).astype(f32)
        value = wave(across, point, 1 - part_across) * weight
        synth_ref[pl.ds(start, step), :] = value.astype(bf16)
        point = (start + iota((1, step), 1)).astype(f32)
        plain_ref[:, pl.ds(start, step)] = wave(down, point, 1 - part).astype(bf16)
        return carry

    lax.fori_loop(0, NPHI // step, body, 0)


def prepare_kernel(
    orders_ref, row_ref, base_hbm, radius_ref, radial_hbm,
    synth_ref, plain_ref, straight_ref, linear_ref, gain_ref,
    base_ref, radial_ref, low_ref, sems
):
    arrivals = [
        pltpu.make_async_copy(base_hbm, base_ref, sems.at[0]),
        pltpu.make_async_copy(radial_hbm, radial_ref, sems.at[1]),
    ]
    for arrival in arrivals:
        arrival.start()
    trig_tables(row_ref[...], synth_ref, plain_ref)
    for arrival in arrivals:
        arrival.wait()
    degrees, columns = base_ref.shape
    shells = columns // 4
    shell, column = iota((shells, columns), 0), iota((shells, columns), 1)
    home = column >> 2 == shell
    spread = [as_ones(home & ((column >> 1) & 1 == f)) for f in range(2)]
    row, column = iota((4 * LANES, columns), 0), iota((4 * LANES, columns), 1)
    same = row & 3 == column & 3
    grow = as_ones(iota((4 * LANES, LANES), 0) >> 2 == iota((4 * LANES, LANES), 1))
    high = radial_ref[...].astype(bf16)
    low = (radial_ref[...] - high.astype(f32)).astype(bf16)
    for term, out_ref in ((high, straight_ref), (low, low_ref)):
        wide = over_degrees(term[0], spread[0]) + over_degrees(term[1], spread[1])
        wide = wide.astype(bf16)
        for q in range(shells // LANES):
            tall = jnp.dot(grow, wide[LANES * q : LANES * (q + 1)], preferred_element_type=f32)
            out_ref[pl.ds(4 * LANES * q, 4 * LANES), :] = jnp.where(same, tall, 0.0).astype(bf16)
    radius = radius_ref[...]
    square = jnp.dot(
        radius * radius, jnp.where(home, 1.0, 0.0), precision=lax.Precision.HIGHEST,
        preferred_element_type=f32,
    )
    order = orders_ref[lax.axis_index("lm")]
    local = lax.axis_index("phi") * degrees + iota((degrees, 1), 0)
    degree = local.astype(f32)
    viscosity = 1.0 / (LMAX * (LMAX + 1.0))
    damping = 1.0 / (1.0 + time_step * viscosity * degree * (degree + 1.0) / square)
    damping = jnp.where(local >= order, damping, 0.0)
    gain_ref[...] = time_step * damping
    factor = time_step * rotation * order.astype(f32) / (degree + 1.0)
    row, column = iota((BLOCK, BLOCK), 0), iota((BLOCK, BLOCK), 1)
    turn = jnp.where(row == column ^ 3, jnp.where(column & 1 == 0, -1.0, 1.0), 0.0).astype(bf16)
    spin = [
        jnp.dot(base_ref[:, BLOCK * q : BLOCK * (q + 1)], turn, preferred_element_type=f32)
        for q in range(columns // BLOCK)
    ]
    stepped = base_ref[...].astype(f32) + factor * jnp.concatenate(spin, 1)
    high = stepped.astype(bf16)
    low = (stepped - high.astype(f32)).astype(bf16)
    linear = jnp.dot(high, straight_ref[...], preferred_element_type=f32)
    linear = linear + jnp.dot(low, straight_ref[...], preferred_element_type=f32)
    linear = linear + jnp.dot(high, low_ref[...], preferred_element_type=f32)
    linear_ref[...] = linear * damping


def masked_rows(orders_ref, legendre_ref, shift, first, count):
    start = lax.rem(lax.axis_index("phi") + shift, 4) * (legendre_ref.shape[0] // 4) + first
    rows = legendre_ref[pl.ds(pl.multiple_of(start, 128), count), :]
    degree = start + lax.broadcasted_iota(jnp.int32, rows.shape, 0)
    order = orders_ref[lax.axis_index("lm")]
    return jnp.where(degree >= order, rows.astype(f32), 0.0).astype(bf16)


def over_degrees(piece, rows):
    return lax.dot_general(piece, rows, (((0,), (0,)), ((), ())), preferred_element_type=f32)


def near_kernel(orders_ref, legendre_ref, base_ref, below_ref, above_ref, out_ref):
    rows = functools.partial(masked_rows, orders_ref, legendre_ref)
    count = base_ref.shape[0]
    total = over_degrees(base_ref[...], rows(0, 0, count))
    total = total + over_degrees(below_ref[...], rows(3, 0, count))
    out_ref[...] = total + over_degrees(above_ref[...], rows(1, 0, count))


def far_kernel(orders_ref, legendre_ref, top_ref, bottom_ref, near_ref, out_hbm, out_ref, sems):
    half = top_ref.shape[0]
    rows = masked_rows(orders_ref, legendre_ref, 2, 0, 2 * half)
    departures = []
    for n in range(out_ref.shape[0] // BLOCK):
        block = pl.ds(BLOCK * n, BLOCK)
        piece = jnp.concatenate([top_ref[:, block], bottom_ref[:, block]], 0)
        out_ref[block, :] = (near_ref[block, :] + over_degrees(piece, rows)).astype(bf16)
        departures.append(pltpu.make_async_copy(out_ref.at[block], out_hbm.at[block], sems.at[n]))
        departures[-1].start()
    for departure in departures:
        departure.wait()


def project_kernel(legendre_ref, weighted_ref, *out_refs, parts):
    turned = weighted_ref[...].T
    for (shift, first), out_ref in zip(parts, out_refs):
        count = out_ref.shape[0]
        start = lax.rem(lax.axis_index("phi") + shift, 4) * (legendre_ref.shape[0] // 4) + first
        rows = legendre_ref[pl.ds(pl.multiple_of(start, 128), count), :]
        out_ref[...] = jnp.dot(rows, turned, preferred_element_type=f32).astype(out_ref.dtype)


def final_kernel(
    own_ref, a_ref, b_ref, c_ref, d_ref, radial_ref, linear_ref, gain_ref, out_hbm, out_ref, sems
):
    half = a_ref.shape[0]
    departures = []
    for n, (first, second) in enumerate([(a_ref, b_ref), (c_ref, d_ref)]):
        block = pl.ds(half * n, half)
        total = own_ref[block, :] + first[...].astype(f32) + second[...].astype(f32)
        moved = jnp.dot(total.astype(bf16), radial_ref[...], preferred_element_type=f32)
        out_ref[block, :] = (linear_ref[block, :] + gain_ref[block, :] * moved).astype(bf16)
        departures.append(pltpu.make_async_copy(out_ref.at[block], out_hbm.at[block], sems.at[n]))
        departures[-1].start()
    for departure in departures:
        departure.wait()


def local_call(kernel, name, outs, table, *args, scratch=(), limit=16, far=(), far_out=False):
    vmem = pl.BlockSpec(memory_space=pltpu.VMEM)
    smem = pl.BlockSpec(memory_space=pltpu.SMEM)
    hbm = pl.BlockSpec(memory_space=pl.ANY)
    first = [] if table is None else [table]
    shapes = [jax.ShapeDtypeStruct(shape, dtype) for shape, dtype in outs]
    return pl.pallas_call(
        kernel,
        out_shape=shapes,
        in_specs=[smem] * len(first) + [hbm if n in far else vmem for n in range(len(args))],
        out_specs=[hbm if far_out else vmem] * len(shapes),
        scratch_shapes=scratch,
        compiler_params=pltpu.CompilerParams(vmem_limit_bytes=limit * 2**20),
        name=name,
    )(*first, *args)


def on_device(spectrum, legendre, orders, quadrature, radius, radial):
    degree_dev, _, columns = spectrum.shape
    ring = lax.axis_size("phi")
    group = lax.axis_size("lm")
    half = degree_dev // 2
    right = [(i, (i + 1) % ring) for i in range(ring)]
    left = [(i, (i - 1) % ring) for i in range(ring)]

    def go(x, way):
        return lax.ppermute(x, "phi", way)

    base = spectrum.reshape(degree_dev, columns)
    table = legendre.reshape(legendre.shape[0], legendre.shape[2])
    rows = table.shape[1]
    below = go(base, right)
    above = go(base, left)
    prepared = local_call(
        prepare_kernel, "prepare",
        [
            ((NPHI, 2 * group), bf16), ((2 * group, NPHI), bf16), ((columns, columns), bf16),
            ((degree_dev, columns), f32), ((degree_dev, columns), f32),
        ],
        orders, orders.reshape(1, group), base, radius.reshape(1, -1), radial,
        scratch=[
            pltpu.VMEM(base.shape, bf16), pltpu.VMEM(radial.shape, f32),
            pltpu.VMEM((columns, columns), bf16), pltpu.SemaphoreType.DMA((2,)),
        ],
        limit=58, far=(1, 3),
    )
    below, above, *prepared = lax.optimization_barrier((below, above, *prepared))
    synth, plain, straight, linear, gain = prepared
    far_top = go(below[:half], right)
    far_bottom = go(above[half:], left)
    (near,) = local_call(
        near_kernel, "near", [((columns, rows), f32)], orders, table, base, below, above
    )
    (latitude,) = local_call(
        far_kernel, "far", [((columns, rows), bf16)], orders, table, far_top, far_bottom, near,
        scratch=[
            pltpu.VMEM((columns, rows), bf16), pltpu.SemaphoreType.DMA((columns // BLOCK,))
        ],
        far_out=True,
    )

    def swap(x):
        x = x.reshape(group, columns // group, rows)
        x = lax.all_to_all(x, "lm", split_axis=0, concat_axis=0, tiled=True)
        return x.reshape(columns, rows)

    weighted = swap(
        grid_call(swap(latitude), synth, plain, quadrature.reshape(1, rows), columns // group // 2, group)
    )

    def project(*parts):
        return local_call(
            functools.partial(project_kernel, parts=[part[:2] for part in parts]),
            "project", [((part[2], columns), part[3]) for part in parts], None, table, weighted,
        )

    far_top, far_bottom = project((2, 0, half, bf16), (2, half, half, bf16))
    from_left = go(far_top, right)
    from_right = go(far_bottom, left)
    above_bottom, below_top, above_top, below_bottom, own = project(
        (1, half, half, bf16), (3, 0, half, bf16), (1, 0, half, f32), (3, half, half, f32),
        (0, 0, degree_dev, f32),
    )
    sum_bottom = go(above_bottom, right)
    sum_top_left = go(below_top, left)
    sum_top = go((above_top + from_left.astype(f32)).astype(bf16), right)
    sum_bottom_left = go((below_bottom + from_right.astype(f32)).astype(bf16), left)
    (result,) = local_call(
        final_kernel, "final", [((degree_dev, columns), bf16)], None, own,
        sum_top, sum_top_left, sum_bottom, sum_bottom_left, straight, linear, gain,
        scratch=[pltpu.VMEM((degree_dev, columns), bf16), pltpu.SemaphoreType.DMA((2,))],
        far_out=True,
    )
    return result.reshape(degree_dev, 1, columns)


def solution(mesh):
    return jax.shard_map(
        on_device,
        mesh=mesh,
        in_specs=(P("phi", "lm", None), P(None, "lm", "phi"), P(), P("phi"), P(), P()),
        out_specs=P("phi", "lm", None),
        check_vma=False,
    )
```

```python
import functools
import math

import jax
import jax.numpy as jnp
from jax import lax
from jax.experimental import pallas as pl
from jax.experimental.pallas import tpu as pltpu
from jax.sharding import PartitionSpec as P

LMAX = 1023
NPHI = 3072
LANES = 128
BLOCK = 256

time_step = 0.5
rotation = 2.0

bf16 = jnp.bfloat16
f32 = jnp.float32


def iota(shape, axis):
    return lax.broadcasted_iota(jnp.int32, shape, axis)


def permutation():
    row, column = iota((BLOCK, BLOCK), 0), iota((BLOCK, BLOCK), 1)
    perm = column == (row & 15) * 16 + 2 * (row >> 5) + ((row >> 4) & 1)
    back = row == (column & 15) * 16 + 2 * (column >> 5) + ((column >> 4) & 1)
    return as_ones(perm), as_ones(back)


def as_ones(mask):
    return jnp.where(mask, 1.0, 0.0).astype(bf16)


def grid_kernel(
    x_ref, synth_hbm, plain_hbm, quad_ref, y_ref,
    synth_ref, plain_ref, a_ref, product_ref, sems, *, step, orders
):
    arrivals = [
        pltpu.make_async_copy(src, dst, sems.at[n])
        for n, (src, dst) in enumerate([(synth_hbm, synth_ref), (plain_hbm, plain_ref)])
    ]
    for arrival in arrivals:
        arrival.start()
    blocks = x_ref.shape[0] // BLOCK
    rows = x_ref.shape[1]
    tiles = [(s, t) for s in range(a_ref.shape[0] // (rows // LANES)) for t in range(rows // LANES)]
    fields = 2 * len(tiles) // (rows // LANES)
    width = BLOCK // fields
    perm, back = permutation()
    quads = quad_ref[...].reshape(1, rows)
    turned = [
        jnp.dot(perm, x_ref[pl.ds(BLOCK * b, BLOCK), :], preferred_element_type=f32).astype(bf16)
        for b in range(blocks)
    ]
    for j, (s, t) in enumerate(tiles):
        for f in range(2):
            first = width * (2 * s + f)
            for b in range(blocks):
                a_ref[j, pl.ds(width * b, width), pl.ds(LANES * f, LANES)] = turned[b][
                    first : first + width, LANES * t : LANES * (t + 1)
                ]
    for arrival in arrivals:
        arrival.wait()
    scale = f32(math.sqrt(orders) / NPHI)
    signed = jnp.where(iota((LANES, 1), 0) & 16 == 0, scale, -scale)
    done = []
    for j, (s, t) in enumerate(tiles):
        slot = j % 2
        for n in range(NPHI // step):
            points = pl.ds(step * n, step)
            grid = jnp.dot(synth_ref[points, :], a_ref[j], preferred_element_type=f32)
            pol, tor = grid[:, :LANES], grid[:, LANES:]
            product_ref[slot, points, pl.ds(0, LANES)] = (pol * tor).astype(bf16)
            product_ref[slot, points, pl.ds(LANES, LANES)] = (pol * pol - tor * tor).astype(bf16)
        part = jnp.dot(plain_ref[...], product_ref[slot], preferred_element_type=f32)
        spectral = (part * signed).astype(bf16).astype(f32)
        quad = quads[:, LANES * t : LANES * (t + 1)]
        done.append((spectral * jnp.concatenate([quad, quad], 1)).astype(bf16))
    for b in range(blocks):
        strips = []
        for t in range(rows // LANES):
            strips.append(
                jnp.concatenate(
                    [
                        done[j][width * b : width * (b + 1), LANES * f : LANES * (f + 1)]
                        for j, (s, at) in enumerate(tiles) if at == t
                        for f in range(2)
                    ],
                    0,
                )
            )
        block = pl.ds(BLOCK * b, BLOCK)
        part = jnp.concatenate(strips, 1)
        y_ref[block, :] = jnp.dot(back, part, preferred_element_type=f32).astype(bf16)


def grid_call(x, synth, plain, quad, fields, orders):
    rows = x.shape[1]
    anywhere = pl.BlockSpec(memory_space=pltpu.HBM)
    vmem = pl.BlockSpec(memory_space=pltpu.VMEM)
    return pl.pallas_call(
        functools.partial(grid_kernel, step=512, orders=orders),
        out_shape=jax.ShapeDtypeStruct(x.shape, bf16),
        in_specs=[vmem, anywhere, anywhere, vmem],
        out_specs=vmem,
        scratch_shapes=[
            pltpu.VMEM(synth.shape, bf16),
            pltpu.VMEM(plain.shape, bf16),
            pltpu.VMEM((fields // 2 * rows // LANES, LANES, 2 * LANES), bf16),
            pltpu.VMEM((2, NPHI, 2 * LANES), bf16),
            pltpu.SemaphoreType.DMA((2,)),
        ],
        compiler_params=pltpu.CompilerParams(vmem_limit_bytes=24 * 2**20),
        name="grid",
    )(x, synth, plain, quad)


def wave(order, point, turn):
    product = order * point
    quarter = jnp.floor(product * f32(4.0 / NPHI) + f32(0.5))
    angle = (product - quarter * f32(NPHI / 4)) * f32(2.0 * math.pi / NPHI)
    square = angle * angle
    sine = angle * (1.0 + square * (-1 / 6 + square * (1 / 120 + square * (-1 / 5040))))
    cosine = 1.0 + square * (-0.5 + square * (1 / 24 + square * (-1 / 720 + square * (1 / 40320))))
    turns = quarter.astype(jnp.int32) + turn
    value = jnp.where(turns & 1 == 1, cosine, sine)
    return jnp.where(turns & 2 == 2, -value, value)


def trig_tables(orders, synth_ref, plain_ref, step=512):
    total = orders.shape[1]
    values = orders.astype(f32)
    picked = iota((2 * total, total), 0)
    picked = (picked >> 5) * 16 + (picked & 15) == iota((2 * total, total), 1)
    down = jnp.sum(jnp.where(picked, values, 0.0), axis=1, keepdims=True)
    diagonal = iota((total, total), 0) == iota((total, total), 1)
    column = jnp.sum(jnp.where(diagonal, values, 0.0), axis=1, keepdims=True)
    picked = iota((total, 2 * total), 1)
    picked = (picked >> 5) * 16 + (picked & 15) == iota((total, 2 * total), 0)
    across = jnp.sum(jnp.where(picked, column, 0.0), axis=0, keepdims=True)
    part = (iota((2 * total, 1), 0) >> 4) & 1
    part_across = (iota((1, 2 * total), 1) >> 4) & 1
    weight = jnp.where(across == 0, 1.0, 2.0) / f32(math.sqrt(total))
    weight = jnp.where(part_across == 0, weight, -weight)

    def body(i, carry):
        start = pl.multiple_of(i * step, step)
        point = (start + iota((step, 1), 0)).astype(f32)
        value = wave(across, point, 1 - part_across) * weight
        synth_ref[pl.ds(start, step), :] = value.astype(bf16)
        point = (start + iota((1, step), 1)).astype(f32)
        plain_ref[:, pl.ds(start, step)] = wave(down, point, 1 - part).astype(bf16)
        return carry

    lax.fori_loop(0, NPHI // step, body, 0)


def prepare_kernel(
    orders_ref, row_ref, base_hbm, radius_ref, radial_hbm,
    synth_ref, plain_ref, straight_ref, linear_ref, gain_ref,
    base_ref, radial_ref, low_ref, sems
):
    arrivals = [
        pltpu.make_async_copy(base_hbm, base_ref, sems.at[0]),
        pltpu.make_async_copy(radial_hbm, radial_ref, sems.at[1]),
    ]
    for arrival in arrivals:
        arrival.start()
    trig_tables(row_ref[...], synth_ref, plain_ref)
    for arrival in arrivals:
        arrival.wait()
    degrees, columns = base_ref.shape
    shells = columns // 4
    shell, column = iota((shells, columns), 0), iota((shells, columns), 1)
    home = column >> 2 == shell
    spread = [as_ones(home & ((column >> 1) & 1 == f)) for f in range(2)]
    row, column = iota((4 * LANES, columns), 0), iota((4 * LANES, columns), 1)
    same = row & 3 == column & 3
    grow = as_ones(iota((4 * LANES, LANES), 0) >> 2 == iota((4 * LANES, LANES), 1))
    high = radial_ref[...].astype(bf16)
    low = (radial_ref[...] - high.astype(f32)).astype(bf16)
    for term, out_ref in ((high, straight_ref), (low, low_ref)):
        wide = over_degrees(term[0], spread[0]) + over_degrees(term[1], spread[1])
        wide = wide.astype(bf16)
        for q in range(shells // LANES):
            tall = jnp.dot(grow, wide[LANES * q : LANES * (q + 1)], preferred_element_type=f32)
            out_ref[pl.ds(4 * LANES * q, 4 * LANES), :] = jnp.where(same, tall, 0.0).astype(bf16)
    radius = radius_ref[...]
    square = jnp.dot(
        radius * radius, jnp.where(home, 1.0, 0.0), precision=lax.Precision.HIGHEST,
        preferred_element_type=f32,
    )
    order = orders_ref[lax.axis_index("lm")]
    local = lax.axis_index("phi") * degrees + iota((degrees, 1), 0)
    degree = local.astype(f32)
    viscosity = 1.0 / (LMAX * (LMAX + 1.0))
    damping = 1.0 / (1.0 + time_step * viscosity * degree * (degree + 1.0) / square)
    damping = jnp.where(local >= order, damping, 0.0)
    gain_ref[...] = time_step * damping
    factor = time_step * rotation * order.astype(f32) / (degree + 1.0)
    row, column = iota((BLOCK, BLOCK), 0), iota((BLOCK, BLOCK), 1)
    turn = jnp.where(row == column ^ 3, jnp.where(column & 1 == 0, -1.0, 1.0), 0.0).astype(bf16)
    spin = [
        jnp.dot(base_ref[:, BLOCK * q : BLOCK * (q + 1)], turn, preferred_element_type=f32)
        for q in range(columns // BLOCK)
    ]
    stepped = base_ref[...].astype(f32) + factor * jnp.concatenate(spin, 1)
    high = stepped.astype(bf16)
    low = (stepped - high.astype(f32)).astype(bf16)
    linear = jnp.dot(high, straight_ref[...], preferred_element_type=f32)
    linear = linear + jnp.dot(low, straight_ref[...], preferred_element_type=f32)
    linear = linear + jnp.dot(high, low_ref[...], preferred_element_type=f32)
    linear_ref[...] = linear * damping


def masked_rows(orders_ref, legendre_ref, shift, first, count):
    start = lax.rem(lax.axis_index("phi") + shift, 4) * (legendre_ref.shape[0] // 4) + first
    rows = legendre_ref[pl.ds(pl.multiple_of(start, 128), count), :]
    degree = start + lax.broadcasted_iota(jnp.int32, rows.shape, 0)
    order = orders_ref[lax.axis_index("lm")]
    return jnp.where(degree >= order, rows.astype(f32), 0.0).astype(bf16)


def over_degrees(piece, rows):
    return lax.dot_general(piece, rows, (((0,), (0,)), ((), ())), preferred_element_type=f32)


def near_kernel(orders_ref, legendre_ref, base_ref, below_ref, above_ref, out_ref):
    rows = functools.partial(masked_rows, orders_ref, legendre_ref)
    count = base_ref.shape[0]
    total = over_degrees(base_ref[...], rows(0, 0, count))
    total = total + over_degrees(below_ref[...], rows(3, 0, count))
    out_ref[...] = total + over_degrees(above_ref[...], rows(1, 0, count))


def far_kernel(orders_ref, legendre_ref, top_ref, bottom_ref, near_ref, out_ref):
    half = top_ref.shape[0]
    rows = masked_rows(orders_ref, legendre_ref, 2, 0, 2 * half)
    for n in range(out_ref.shape[0] // BLOCK):
        block = pl.ds(BLOCK * n, BLOCK)
        piece = jnp.concatenate([top_ref[:, block], bottom_ref[:, block]], 0)
        out_ref[block, :] = (near_ref[block, :] + over_degrees(piece, rows)).astype(bf16)


def project_kernel(legendre_ref, weighted_ref, *out_refs, parts):
    turned = weighted_ref[...].T
    for (shift, first), out_ref in zip(parts, out_refs):
        count = out_ref.shape[0]
        start = lax.rem(lax.axis_index("phi") + shift, 4) * (legendre_ref.shape[0] // 4) + first
        rows = legendre_ref[pl.ds(pl.multiple_of(start, 128), count), :]
        out_ref[...] = jnp.dot(rows, turned, preferred_element_type=f32).astype(out_ref.dtype)


def final_kernel(
    own_ref, a_ref, b_ref, c_ref, d_ref, radial_ref, linear_ref, gain_ref, out_hbm, out_ref, sems
):
    half = a_ref.shape[0]
    departures = []
    for n, (first, second) in enumerate([(a_ref, b_ref), (c_ref, d_ref)]):
        block = pl.ds(half * n, half)
        total = own_ref[block, :] + first[...].astype(f32) + second[...].astype(f32)
        moved = jnp.dot(total.astype(bf16), radial_ref[...], preferred_element_type=f32)
        out_ref[block, :] = (linear_ref[block, :] + gain_ref[block, :] * moved).astype(bf16)
        departures.append(pltpu.make_async_copy(out_ref.at[block], out_hbm.at[block], sems.at[n]))
        departures[-1].start()
    for departure in departures:
        departure.wait()


def local_call(kernel, name, outs, table, *args, scratch=(), limit=16, far=(), far_out=False):
    vmem = pl.BlockSpec(memory_space=pltpu.VMEM)
    smem = pl.BlockSpec(memory_space=pltpu.SMEM)
    hbm = pl.BlockSpec(memory_space=pl.ANY)
    first = [] if table is None else [table]
    shapes = [jax.ShapeDtypeStruct(shape, dtype) for shape, dtype in outs]
    return pl.pallas_call(
        kernel,
        out_shape=shapes,
        in_specs=[smem] * len(first) + [hbm if n in far else vmem for n in range(len(args))],
        out_specs=[hbm if far_out else vmem] * len(shapes),
        scratch_shapes=scratch,
        compiler_params=pltpu.CompilerParams(vmem_limit_bytes=limit * 2**20),
        name=name,
    )(*first, *args)


def on_device(spectrum, legendre, orders, quadrature, radius, radial):
    degree_dev, _, columns = spectrum.shape
    ring = lax.axis_size("phi")
    group = lax.axis_size("lm")
    half = degree_dev // 2
    right = [(i, (i + 1) % ring) for i in range(ring)]
    left = [(i, (i - 1) % ring) for i in range(ring)]

    def go(x, way):
        return lax.ppermute(x, "phi", way)

    base = spectrum.reshape(degree_dev, columns)
    table = legendre.reshape(legendre.shape[0], legendre.shape[2])
    rows = table.shape[1]
    below = go(base, right)
    above = go(base, left)
    prepared = local_call(
        prepare_kernel, "prepare",
        [
            ((NPHI, 2 * group), bf16), ((2 * group, NPHI), bf16), ((columns, columns), bf16),
            ((degree_dev, columns), f32), ((degree_dev, columns), f32),
        ],
        orders, orders.reshape(1, group), base, radius.reshape(1, -1), radial,
        scratch=[
            pltpu.VMEM(base.shape, bf16), pltpu.VMEM(radial.shape, f32),
            pltpu.VMEM((columns, columns), bf16), pltpu.SemaphoreType.DMA((2,)),
        ],
        limit=60, far=(1, 3),
    )
    below, above, *prepared = lax.optimization_barrier((below, above, *prepared))
    synth, plain, straight, linear, gain = prepared
    far_top = go(below[:half], right)
    far_bottom = go(above[half:], left)
    (near,) = local_call(
        near_kernel, "near", [((columns, rows), f32)], orders, table, base, below, above
    )
    (latitude,) = local_call(
        far_kernel, "far", [((columns, rows), bf16)], orders, table, far_top, far_bottom, near,
    )

    def swap(x):
        x = x.reshape(group, columns // group, rows)
        x = lax.all_to_all(x, "lm", split_axis=0, concat_axis=0, tiled=True)
        return x.reshape(columns, rows)

    weighted = swap(
        grid_call(swap(latitude), synth, plain, quadrature, columns // group // 2, group)
    )

    def project(*parts):
        return local_call(
            functools.partial(project_kernel, parts=[part[:2] for part in parts]),
            "project", [((part[2], columns), part[3]) for part in parts], None, table, weighted,
        )

    far_top, far_bottom = project((2, 0, half, bf16), (2, half, half, bf16))
    from_left = go(far_top, right)
    from_right = go(far_bottom, left)
    above_bottom, below_top, above_top, below_bottom, own = project(
        (1, half, half, bf16), (3, 0, half, bf16), (1, 0, half, f32), (3, half, half, f32),
        (0, 0, degree_dev, f32),
    )
    sum_bottom = go(above_bottom, right)
    sum_top_left = go(below_top, left)
    sum_top = go((above_top + from_left.astype(f32)).astype(bf16), right)
    sum_bottom_left = go((below_bottom + from_right.astype(f32)).astype(bf16), left)
    (result,) = local_call(
        final_kernel, "final", [((degree_dev, columns), bf16)], None, own,
        sum_top, sum_top_left, sum_bottom, sum_bottom_left, straight, linear, gain,
        scratch=[pltpu.VMEM((degree_dev, columns), bf16), pltpu.SemaphoreType.DMA((2,))],
        far_out=True,
    )
    return result.reshape(degree_dev, 1, columns)


def solution(mesh):
    return jax.shard_map(
        on_device,
        mesh=mesh,
        in_specs=(P("phi", "lm", None), P(None, "lm", "phi"), P(), P("phi"), P(), P()),
        out_specs=P("phi", "lm", None),
        check_vma=False,
    )
```

```python
import functools
import math

import jax
import jax.numpy as jnp
from jax import lax
from jax.experimental import pallas as pl
from jax.experimental.pallas import tpu as pltpu
from jax.sharding import PartitionSpec as P

LMAX = 1023
NPHI = 3072
LANES = 128
BLOCK = 256

time_step = 0.5
rotation = 2.0

bf16 = jnp.bfloat16
f32 = jnp.float32


def iota(shape, axis):
    return lax.broadcasted_iota(jnp.int32, shape, axis)


def permutation():
    row, column = iota((BLOCK, BLOCK), 0), iota((BLOCK, BLOCK), 1)
    perm = column == (row & 15) * 16 + 2 * (row >> 5) + ((row >> 4) & 1)
    back = row == (column & 15) * 16 + 2 * (column >> 5) + ((column >> 4) & 1)
    return as_ones(perm), as_ones(back)


def as_ones(mask):
    return jnp.where(mask, 1.0, 0.0).astype(bf16)


def grid_kernel(
    x_ref, synth_hbm, plain_hbm, quad_ref, y_ref,
    synth_ref, plain_ref, a_ref, product_ref, sems, *, step, orders
):
    arrivals = [
        pltpu.make_async_copy(src, dst, sems.at[n])
        for n, (src, dst) in enumerate([(synth_hbm, synth_ref), (plain_hbm, plain_ref)])
    ]
    for arrival in arrivals:
        arrival.start()
    blocks = x_ref.shape[0] // BLOCK
    rows = x_ref.shape[1]
    tiles = [(s, t) for s in range(a_ref.shape[0] // (rows // LANES)) for t in range(rows // LANES)]
    fields = 2 * len(tiles) // (rows // LANES)
    width = BLOCK // fields
    perm, back = permutation()
    quads = quad_ref[...].reshape(1, rows)
    turned = [
        jnp.dot(perm, x_ref[pl.ds(BLOCK * b, BLOCK), :], preferred_element_type=f32).astype(bf16)
        for b in range(blocks)
    ]
    for j, (s, t) in enumerate(tiles):
        for f in range(2):
            first = width * (2 * s + f)
            for b in range(blocks):
                a_ref[j, pl.ds(width * b, width), pl.ds(LANES * f, LANES)] = turned[b][
                    first : first + width, LANES * t : LANES * (t + 1)
                ]
    for arrival in arrivals:
        arrival.wait()
    scale = f32(math.sqrt(orders) / NPHI)
    signed = jnp.where(iota((LANES, 1), 0) & 16 == 0, scale, -scale)
    done = []
    for j, (s, t) in enumerate(tiles):
        slot = j % 2
        for n in range(NPHI // step):
            points = pl.ds(step * n, step)
            grid = jnp.dot(synth_ref[points, :], a_ref[j], preferred_element_type=f32)
            pol, tor = grid[:, :LANES], grid[:, LANES:]
            product_ref[slot, points, pl.ds(0, LANES)] = (pol * tor).astype(bf16)
            product_ref[slot, points, pl.ds(LANES, LANES)] = (pol * pol - tor * tor).astype(bf16)
        part = jnp.dot(plain_ref[...], product_ref[slot], preferred_element_type=f32)
        spectral = (part * signed).astype(bf16).astype(f32)
        quad = quads[:, LANES * t : LANES * (t + 1)]
        done.append((spectral * jnp.concatenate([quad, quad], 1)).astype(bf16))
    for b in range(blocks):
        strips = []
        for t in range(rows // LANES):
            strips.append(
                jnp.concatenate(
                    [
                        done[j][width * b : width * (b + 1), LANES * f : LANES * (f + 1)]
                        for j, (s, at) in enumerate(tiles) if at == t
                        for f in range(2)
                    ],
                    0,
                )
            )
        block = pl.ds(BLOCK * b, BLOCK)
        part = jnp.concatenate(strips, 1)
        y_ref[block, :] = jnp.dot(back, part, preferred_element_type=f32).astype(bf16)


def grid_call(x, synth, plain, quad, fields, orders):
    rows = x.shape[1]
    anywhere = pl.BlockSpec(memory_space=pltpu.HBM)
    vmem = pl.BlockSpec(memory_space=pltpu.VMEM)
    return pl.pallas_call(
        functools.partial(grid_kernel, step=512, orders=orders),
        out_shape=jax.ShapeDtypeStruct(x.shape, bf16),
        in_specs=[vmem, anywhere, anywhere, vmem],
        out_specs=vmem,
        scratch_shapes=[
            pltpu.VMEM(synth.shape, bf16),
            pltpu.VMEM(plain.shape, bf16),
            pltpu.VMEM((fields // 2 * rows // LANES, LANES, 2 * LANES), bf16),
            pltpu.VMEM((2, NPHI, 2 * LANES), bf16),
            pltpu.SemaphoreType.DMA((2,)),
        ],
        compiler_params=pltpu.CompilerParams(vmem_limit_bytes=24 * 2**20),
        name="grid",
    )(x, synth, plain, quad)


def wave(order, point, turn):
    product = order * point
    quarter = jnp.floor(product * f32(4.0 / NPHI) + f32(0.5))
    angle = (product - quarter * f32(NPHI / 4)) * f32(2.0 * math.pi / NPHI)
    square = angle * angle
    sine = angle * (1.0 + square * (-1 / 6 + square * (1 / 120 + square * (-1 / 5040))))
    cosine = 1.0 + square * (-0.5 + square * (1 / 24 + square * (-1 / 720 + square * (1 / 40320))))
    turns = quarter.astype(jnp.int32) + turn
    value = jnp.where(turns & 1 == 1, cosine, sine)
    return jnp.where(turns & 2 == 2, -value, value)


def trig_tables(orders, synth_ref, plain_ref, step=512):
    total = orders.shape[1]
    values = orders.astype(f32)
    picked = iota((2 * total, total), 0)
    picked = (picked >> 5) * 16 + (picked & 15) == iota((2 * total, total), 1)
    down = jnp.sum(jnp.where(picked, values, 0.0), axis=1, keepdims=True)
    diagonal = iota((total, total), 0) == iota((total, total), 1)
    column = jnp.sum(jnp.where(diagonal, values, 0.0), axis=1, keepdims=True)
    picked = iota((total, 2 * total), 1)
    picked = (picked >> 5) * 16 + (picked & 15) == iota((total, 2 * total), 0)
    across = jnp.sum(jnp.where(picked, column, 0.0), axis=0, keepdims=True)
    part = (iota((2 * total, 1), 0) >> 4) & 1
    part_across = (iota((1, 2 * total), 1) >> 4) & 1
    weight = jnp.where(across == 0, 1.0, 2.0) / f32(math.sqrt(total))
    weight = jnp.where(part_across == 0, weight, -weight)

    def body(i, carry):
        start = pl.multiple_of(i * step, step)
        point = (start + iota((step, 1), 0)).astype(f32)
        value = wave(across, point, 1 - part_across) * weight
        synth_ref[pl.ds(start, step), :] = value.astype(bf16)
        point = (start + iota((1, step), 1)).astype(f32)
        plain_ref[:, pl.ds(start, step)] = wave(down, point, 1 - part).astype(bf16)
        return carry

    lax.fori_loop(0, NPHI // step, body, 0)


def prepare_kernel(
    orders_ref, row_ref, base_hbm, radius_ref, radial_hbm,
    synth_ref, plain_ref, straight_ref, linear_ref, gain_ref,
    base_ref, radial_ref, low_ref, sems
):
    arrivals = [
        pltpu.make_async_copy(base_hbm, base_ref, sems.at[0]),
        pltpu.make_async_copy(radial_hbm, radial_ref, sems.at[1]),
    ]
    for arrival in arrivals:
        arrival.start()
    trig_tables(row_ref[...], synth_ref, plain_ref)
    for arrival in arrivals:
        arrival.wait()
    degrees, columns = base_ref.shape
    shells = columns // 4
    shell, column = iota((shells, columns), 0), iota((shells, columns), 1)
    home = column >> 2 == shell
    spread = [as_ones(home & ((column >> 1) & 1 == f)) for f in range(2)]
    row, column = iota((4 * LANES, columns), 0), iota((4 * LANES, columns), 1)
    same = row & 3 == column & 3
    grow = as_ones(iota((4 * LANES, LANES), 0) >> 2 == iota((4 * LANES, LANES), 1))
    high = radial_ref[...].astype(bf16)
    low = (radial_ref[...] - high.astype(f32)).astype(bf16)
    for term, out_ref in ((high, straight_ref), (low, low_ref)):
        wide = over_degrees(term[0], spread[0]) + over_degrees(term[1], spread[1])
        wide = wide.astype(bf16)
        for q in range(shells // LANES):
            tall = jnp.dot(grow, wide[LANES * q : LANES * (q + 1)], preferred_element_type=f32)
            out_ref[pl.ds(4 * LANES * q, 4 * LANES), :] = jnp.where(same, tall, 0.0).astype(bf16)
    radius = radius_ref[...]
    square = jnp.dot(
        radius * radius, jnp.where(home, 1.0, 0.0), precision=lax.Precision.HIGHEST,
        preferred_element_type=f32,
    )
    order = orders_ref[lax.axis_index("lm")]
    local = lax.axis_index("phi") * degrees + iota((degrees, 1), 0)
    degree = local.astype(f32)
    viscosity = 1.0 / (LMAX * (LMAX + 1.0))
    damping = 1.0 / (1.0 + time_step * viscosity * degree * (degree + 1.0) / square)
    damping = jnp.where(local >= order, damping, 0.0)
    gain_ref[...] = time_step * damping
    factor = time_step * rotation * order.astype(f32) / (degree + 1.0)
    row, column = iota((BLOCK, BLOCK), 0), iota((BLOCK, BLOCK), 1)
    turn = jnp.where(row == column ^ 3, jnp.where(column & 1 == 0, -1.0, 1.0), 0.0).astype(bf16)
    spin = [
        jnp.dot(base_ref[:, BLOCK * q : BLOCK * (q + 1)], turn, preferred_element_type=f32)
        for q in range(columns // BLOCK)
    ]
    stepped = base_ref[...].astype(f32) + factor * jnp.concatenate(spin, 1)
    high = stepped.astype(bf16)
    low = (stepped - high.astype(f32)).astype(bf16)
    linear = jnp.dot(high, straight_ref[...], preferred_element_type=f32)
    linear = linear + jnp.dot(low, straight_ref[...], preferred_element_type=f32)
    linear = linear + jnp.dot(high, low_ref[...], preferred_element_type=f32)
    linear_ref[...] = linear * damping


def masked_rows(orders_ref, legendre_ref, shift, first, count):
    start = lax.rem(lax.axis_index("phi") + shift, 4) * (legendre_ref.shape[0] // 4) + first
    rows = legendre_ref[pl.ds(pl.multiple_of(start, 128), count), :]
    degree = start + lax.broadcasted_iota(jnp.int32, rows.shape, 0)
    order = orders_ref[lax.axis_index("lm")]
    return jnp.where(degree >= order, rows.astype(f32), 0.0).astype(bf16)


def over_degrees(piece, rows):
    return lax.dot_general(piece, rows, (((0,), (0,)), ((), ())), preferred_element_type=f32)


def near_kernel(orders_ref, legendre_ref, base_ref, below_ref, above_ref, out_ref):
    rows = functools.partial(masked_rows, orders_ref, legendre_ref)
    count = base_ref.shape[0]
    total = over_degrees(base_ref[...], rows(0, 0, count))
    total = total + over_degrees(below_ref[...], rows(3, 0, count))
    out_ref[...] = total + over_degrees(above_ref[...], rows(1, 0, count))


def far_kernel(orders_ref, legendre_ref, top_ref, bottom_ref, near_ref, out_ref):
    half = top_ref.shape[0]
    rows = masked_rows(orders_ref, legendre_ref, 2, 0, 2 * half)
    for n in range(out_ref.shape[0] // BLOCK):
        block = pl.ds(BLOCK * n, BLOCK)
        piece = jnp.concatenate([top_ref[:, block], bottom_ref[:, block]], 0)
        out_ref[block, :] = (near_ref[block, :] + over_degrees(piece, rows)).astype(bf16)


def project_kernel(legendre_ref, weighted_ref, *out_refs, parts):
    turned = weighted_ref[...].T
    for (shift, first), out_ref in zip(parts, out_refs):
        count = out_ref.shape[0]
        start = lax.rem(lax.axis_index("phi") + shift, 4) * (legendre_ref.shape[0] // 4) + first
        rows = legendre_ref[pl.ds(pl.multiple_of(start, 128), count), :]
        out_ref[...] = jnp.dot(rows, turned, preferred_element_type=f32).astype(out_ref.dtype)


def final_kernel(
    own_ref, a_ref, b_ref, radial_ref, linear_ref, gain_ref, *refs, first
):
    out_hbm, out_ref, sem = refs[-3:]
    block = pl.ds(first, a_ref.shape[0])
    total = own_ref[block, :] + a_ref[...].astype(f32) + b_ref[...].astype(f32)
    moved = jnp.dot(total.astype(bf16), radial_ref[...], preferred_element_type=f32)
    out_ref[...] = (linear_ref[block, :] + gain_ref[block, :] * moved).astype(bf16)
    departure = pltpu.make_async_copy(out_ref, out_hbm.at[block], sem)
    departure.start()
    departure.wait()


def local_call(kernel, name, outs, table, *args, scratch=(), limit=16, far=(), far_out=False, alias=None):
    vmem = pl.BlockSpec(memory_space=pltpu.VMEM)
    smem = pl.BlockSpec(memory_space=pltpu.SMEM)
    hbm = pl.BlockSpec(memory_space=pl.ANY)
    first = [] if table is None else [table]
    shapes = [jax.ShapeDtypeStruct(shape, dtype) for shape, dtype in outs]
    return pl.pallas_call(
        kernel,
        out_shape=shapes,
        in_specs=[smem] * len(first) + [hbm if n in far else vmem for n in range(len(args))],
        out_specs=[hbm if far_out else vmem] * len(shapes),
        scratch_shapes=scratch,
        input_output_aliases={} if alias is None else {alias: 0},
        compiler_params=pltpu.CompilerParams(vmem_limit_bytes=limit * 2**20),
        name=name,
    )(*first, *args)


def on_device(spectrum, legendre, orders, quadrature, radius, radial):
    degree_dev, _, columns = spectrum.shape
    ring = lax.axis_size("phi")
    group = lax.axis_size("lm")
    half = degree_dev // 2
    right = [(i, (i + 1) % ring) for i in range(ring)]
    left = [(i, (i - 1) % ring) for i in range(ring)]

    def go(x, way):
        return lax.ppermute(x, "phi", way)

    base = spectrum.reshape(degree_dev, columns)
    table = legendre.reshape(legendre.shape[0], legendre.shape[2])
    rows = table.shape[1]
    below = go(base, right)
    above = go(base, left)
    prepared = local_call(
        prepare_kernel, "prepare",
        [
            ((NPHI, 2 * group), bf16), ((2 * group, NPHI), bf16), ((columns, columns), bf16),
            ((degree_dev, columns), f32), ((degree_dev, columns), f32),
        ],
        orders, orders.reshape(1, group), base, radius.reshape(1, -1), radial,
        scratch=[
            pltpu.VMEM(base.shape, bf16), pltpu.VMEM(radial.shape, f32),
            pltpu.VMEM((columns, columns), bf16), pltpu.SemaphoreType.DMA((2,)),
        ],
        limit=60, far=(1, 3),
    )
    below, *prepared = lax.optimization_barrier((below, *prepared))
    synth, plain, straight, linear, gain = prepared
    far_top = go(below[:half], right)
    far_bottom = go(above[half:], left)
    (near,) = local_call(
        near_kernel, "near", [((columns, rows), f32)], orders, table, base, below, above
    )
    (latitude,) = local_call(
        far_kernel, "far", [((columns, rows), bf16)], orders, table, far_top, far_bottom, near,
    )

    def swap(x):
        x = x.reshape(group, columns // group, rows)
        x = lax.all_to_all(x, "lm", split_axis=0, concat_axis=0, tiled=True)
        return x.reshape(columns, rows)

    weighted = swap(
        grid_call(swap(latitude), synth, plain, quadrature, columns // group // 2, group)
    )

    def project(*parts):
        return local_call(
            functools.partial(project_kernel, parts=[part[:2] for part in parts]),
            "project", [((part[2], columns), part[3]) for part in parts], None, table, weighted,
        )

    far_top, far_bottom = project((2, 0, half, bf16), (2, half, half, bf16))
    from_left = go(far_top, right)
    from_right = go(far_bottom, left)
    above_bottom, below_top, above_top, below_bottom, own = project(
        (1, half, half, bf16), (3, 0, half, bf16), (1, 0, half, f32), (3, half, half, f32),
        (0, 0, degree_dev, f32),
    )
    sum_bottom = go(above_bottom, right)
    sum_top_left = go(below_top, left)
    sum_top = go((above_top + from_left.astype(f32)).astype(bf16), right)
    sum_bottom_left = go((below_bottom + from_right.astype(f32)).astype(bf16), left)
    def finish(first, one, two, *held):
        return local_call(
            functools.partial(final_kernel, first=first), "final",
            [((degree_dev, columns), bf16)], None, own, one, two, straight, linear, gain, *held,
            scratch=[pltpu.VMEM((half, columns), bf16), pltpu.SemaphoreType.DMA(())],
            far=(6,), far_out=True, alias=6 if held else None,
        )

    (result,) = finish(half, sum_bottom, sum_bottom_left)
    (result,) = finish(0, sum_top, sum_top_left, result)
    return result.reshape(degree_dev, 1, columns)


def solution(mesh):
    return jax.shard_map(
        on_device,
        mesh=mesh,
        in_specs=(P("phi", "lm", None), P(None, "lm", "phi"), P(), P("phi"), P(), P()),
        out_specs=P("phi", "lm", None),
        check_vma=False,
    )
```

```python
import functools
import math

import jax
import jax.numpy as jnp
from jax import lax
from jax.experimental import pallas as pl
from jax.experimental.pallas import tpu as pltpu
from jax.sharding import PartitionSpec as P

LMAX = 1023
NPHI = 3072
LANES = 128
BLOCK = 256
SHIFT = 32

time_step = 0.5
rotation = 2.0

bf16 = jnp.bfloat16
f32 = jnp.float32


def iota(shape, axis):
    return lax.broadcasted_iota(jnp.int32, shape, axis)


def permutation():
    row, column = iota((BLOCK, BLOCK), 0), iota((BLOCK, BLOCK), 1)
    perm = column == (row & 15) * 16 + 2 * (row >> 5) + ((row >> 4) & 1)
    back = row == (column & 15) * 16 + 2 * (column >> 5) + ((column >> 4) & 1)
    return as_ones(perm), as_ones(back)


def as_ones(mask):
    return jnp.where(mask, 1.0, 0.0).astype(bf16)


def grid_kernel(
    x_ref, synth_hbm, plain_hbm, quad_ref, y_ref,
    synth_ref, plain_ref, a_ref, product_ref, sems, *, step, orders
):
    arrivals = [
        pltpu.make_async_copy(src, dst, sems.at[n])
        for n, (src, dst) in enumerate([(synth_hbm, synth_ref), (plain_hbm, plain_ref)])
    ]
    for arrival in arrivals:
        arrival.start()
    blocks = x_ref.shape[0] // BLOCK
    rows = x_ref.shape[1]
    tiles = [(s, t) for s in range(a_ref.shape[0] // (rows // LANES)) for t in range(rows // LANES)]
    fields = 2 * len(tiles) // (rows // LANES)
    width = BLOCK // fields
    perm, back = permutation()
    quads = quad_ref[...].reshape(1, rows)
    turned = [
        jnp.dot(perm, x_ref[pl.ds(BLOCK * b, BLOCK), :], preferred_element_type=f32).astype(bf16)
        for b in range(blocks)
    ]
    for j, (s, t) in enumerate(tiles):
        for f in range(2):
            first = width * (2 * s + f)
            for b in range(blocks):
                a_ref[j, pl.ds(width * b, width), pl.ds(LANES * f, LANES)] = turned[b][
                    first : first + width, LANES * t : LANES * (t + 1)
                ]
    for arrival in arrivals:
        arrival.wait()
    scale = f32(math.sqrt(orders) / NPHI)
    signed = jnp.where(iota((LANES, 1), 0) & 16 == 0, scale, -scale)
    done = []
    for j, (s, t) in enumerate(tiles):
        slot = j % 2
        for n in range(NPHI // step):
            points = pl.ds(step * n, step)
            grid = jnp.dot(synth_ref[points, :], a_ref[j], preferred_element_type=f32)
            pol, tor = grid[:, :LANES], grid[:, LANES:]
            product_ref[slot, points, pl.ds(0, LANES)] = (pol * tor).astype(bf16)
            product_ref[slot, points, pl.ds(LANES, LANES)] = (pol * pol - tor * tor).astype(bf16)
        part = jnp.dot(plain_ref[...], product_ref[slot], preferred_element_type=f32)
        spectral = (part * signed).astype(bf16).astype(f32)
        quad = quads[:, LANES * t : LANES * (t + 1)]
        done.append((spectral * jnp.concatenate([quad, quad], 1)).astype(bf16))
    for b in range(blocks):
        strips = []
        for t in range(rows // LANES):
            strips.append(
                jnp.concatenate(
                    [
                        done[j][width * b : width * (b + 1), LANES * f : LANES * (f + 1)]
                        for j, (s, at) in enumerate(tiles) if at == t
                        for f in range(2)
                    ],
                    0,
                )
            )
        block = pl.ds(BLOCK * b, BLOCK)
        part = jnp.concatenate(strips, 1)
        y_ref[block, :] = jnp.dot(back, part, preferred_element_type=f32).astype(bf16)


def grid_call(x, synth, plain, quad, fields, orders):
    rows = x.shape[1]
    anywhere = pl.BlockSpec(memory_space=pltpu.HBM)
    vmem = pl.BlockSpec(memory_space=pltpu.VMEM)
    return pl.pallas_call(
        functools.partial(grid_kernel, step=512, orders=orders),
        out_shape=jax.ShapeDtypeStruct(x.shape, bf16),
        in_specs=[vmem, anywhere, anywhere, vmem],
        out_specs=vmem,
        scratch_shapes=[
            pltpu.VMEM(synth.shape, bf16),
            pltpu.VMEM(plain.shape, bf16),
            pltpu.VMEM((fields // 2 * rows // LANES, LANES, 2 * LANES), bf16),
            pltpu.VMEM((2, NPHI, 2 * LANES), bf16),
            pltpu.SemaphoreType.DMA((2,)),
        ],
        compiler_params=pltpu.CompilerParams(vmem_limit_bytes=24 * 2**20),
        name="grid",
    )(x, synth, plain, quad)


def wave(order, point, turn):
    product = order * point
    quarter = jnp.floor(product * f32(4.0 / NPHI) + f32(0.5))
    angle = (product - quarter * f32(NPHI / 4)) * f32(2.0 * math.pi / NPHI)
    square = angle * angle
    sine = angle * (1.0 + square * (-1 / 6 + square * (1 / 120 + square * (-1 / 5040))))
    cosine = 1.0 + square * (-0.5 + square * (1 / 24 + square * (-1 / 720 + square * (1 / 40320))))
    turns = quarter.astype(jnp.int32) + turn
    value = jnp.where(turns & 1 == 1, cosine, sine)
    return jnp.where(turns & 2 == 2, -value, value)


def trig_tables(orders, synth_ref, plain_ref, step=512):
    total = orders.shape[1]
    values = orders.astype(f32)
    picked = iota((2 * total, total), 0)
    picked = (picked >> 5) * 16 + (picked & 15) == iota((2 * total, total), 1)
    down = jnp.sum(jnp.where(picked, values, 0.0), axis=1, keepdims=True)
    diagonal = iota((total, total), 0) == iota((total, total), 1)
    column = jnp.sum(jnp.where(diagonal, values, 0.0), axis=1, keepdims=True)
    picked = iota((total, 2 * total), 1)
    picked = (picked >> 5) * 16 + (picked & 15) == iota((total, 2 * total), 0)
    across = jnp.sum(jnp.where(picked, column, 0.0), axis=0, keepdims=True)
    part = (iota((2 * total, 1), 0) >> 4) & 1
    part_across = (iota((1, 2 * total), 1) >> 4) & 1
    weight = jnp.where(across == 0, 1.0, 2.0) / f32(math.sqrt(total))
    weight = jnp.where(part_across == 0, weight, -weight)

    def body(i, carry):
        start = pl.multiple_of(i * step, step)
        point = (start + iota((step, 1), 0)).astype(f32)
        value = wave(across, point, 1 - part_across) * weight
        synth_ref[pl.ds(start, step), :] = value.astype(bf16)
        point = (start + iota((1, step), 1)).astype(f32)
        plain_ref[:, pl.ds(start, step)] = wave(down, point, 1 - part).astype(bf16)
        return carry

    lax.fori_loop(0, NPHI // step, body, 0)


def prepare_kernel(
    orders_ref, row_ref, base_hbm, radius_ref, radial_hbm,
    synth_ref, plain_ref, straight_ref, linear_ref, gain_ref,
    base_ref, radial_ref, low_ref, sems
):
    arrivals = [
        pltpu.make_async_copy(base_hbm, base_ref, sems.at[0]),
        pltpu.make_async_copy(radial_hbm, radial_ref, sems.at[1]),
    ]
    for arrival in arrivals:
        arrival.start()
    trig_tables(row_ref[...], synth_ref, plain_ref)
    for arrival in arrivals:
        arrival.wait()
    degrees, columns = base_ref.shape
    shells = columns // 4
    shell, column = iota((shells, columns), 0), iota((shells, columns), 1)
    home = column >> 2 == shell
    spread = [as_ones(home & ((column >> 1) & 1 == f)) for f in range(2)]
    row, column = iota((4 * LANES, columns), 0), iota((4 * LANES, columns), 1)
    same = row & 3 == column & 3
    grow = as_ones(iota((4 * LANES, LANES), 0) >> 2 == iota((4 * LANES, LANES), 1))
    high = radial_ref[...].astype(bf16)
    low = (radial_ref[...] - high.astype(f32)).astype(bf16)
    for term, out_ref in ((high, straight_ref), (low, low_ref)):
        wide = over_degrees(term[0], spread[0]) + over_degrees(term[1], spread[1])
        wide = wide.astype(bf16)
        for q in range(shells // LANES):
            tall = jnp.dot(grow, wide[LANES * q : LANES * (q + 1)], preferred_element_type=f32)
            out_ref[pl.ds(4 * LANES * q, 4 * LANES), :] = jnp.where(same, tall, 0.0).astype(bf16)
    radius = radius_ref[...]
    square = jnp.dot(
        radius * radius, jnp.where(home, 1.0, 0.0), precision=lax.Precision.HIGHEST,
        preferred_element_type=f32,
    )
    order = orders_ref[lax.axis_index("lm")]
    local = lax.axis_index("phi") * degrees + iota((degrees, 1), 0)
    degree = local.astype(f32)
    viscosity = 1.0 / (LMAX * (LMAX + 1.0))
    damping = 1.0 / (1.0 + time_step * viscosity * degree * (degree + 1.0) / square)
    damping = jnp.where(local >= order, damping, 0.0)
    gain_ref[...] = time_step * damping
    factor = time_step * rotation * order.astype(f32) / (degree + 1.0)
    row, column = iota((BLOCK, BLOCK), 0), iota((BLOCK, BLOCK), 1)
    turn = jnp.where(row == column ^ 3, jnp.where(column & 1 == 0, -1.0, 1.0), 0.0).astype(bf16)
    spin = [
        jnp.dot(base_ref[:, BLOCK * q : BLOCK * (q + 1)], turn, preferred_element_type=f32)
        for q in range(columns // BLOCK)
    ]
    stepped = base_ref[...].astype(f32) + factor * jnp.concatenate(spin, 1)
    high = stepped.astype(bf16)
    low = (stepped - high.astype(f32)).astype(bf16)
    linear = jnp.dot(high, straight_ref[...], preferred_element_type=f32)
    linear = linear + jnp.dot(low, straight_ref[...], preferred_element_type=f32)
    linear = linear + jnp.dot(high, low_ref[...], preferred_element_type=f32)
    linear_ref[...] = linear * damping


def masked_rows(orders_ref, legendre_ref, shift, first, count):
    start = lax.rem(lax.axis_index("phi") + shift, 4) * (legendre_ref.shape[0] // 4) + first
    rows = legendre_ref[pl.ds(pl.multiple_of(start, 128), count), :]
    degree = start + lax.broadcasted_iota(jnp.int32, rows.shape, 0)
    order = orders_ref[lax.axis_index("lm")]
    return jnp.where(degree >= order, rows.astype(f32), 0.0).astype(bf16)


def over_degrees(piece, rows):
    return lax.dot_general(piece, rows, (((0,), (0,)), ((), ())), preferred_element_type=f32)


def near_kernel(orders_ref, legendre_ref, base_ref, below_ref, above_ref, out_ref):
    rows = functools.partial(masked_rows, orders_ref, legendre_ref)
    count = base_ref.shape[0]
    total = over_degrees(base_ref[...], rows(0, 0, count))
    total = total + over_degrees(below_ref[...], rows(3, 0, count))
    out_ref[...] = total + over_degrees(above_ref[...], rows(1, 0, count))


def far_kernel(orders_ref, legendre_ref, top_ref, bottom_ref, near_ref, out_ref):
    half = top_ref.shape[0]
    rows = masked_rows(orders_ref, legendre_ref, 2, 0, 2 * half)
    for n in range(out_ref.shape[0] // BLOCK):
        block = pl.ds(BLOCK * n, BLOCK)
        piece = jnp.concatenate([top_ref[:, block], bottom_ref[:, block]], 0)
        out_ref[block, :] = (near_ref[block, :] + over_degrees(piece, rows)).astype(bf16)


def project_kernel(legendre_ref, weighted_ref, *out_refs, parts):
    turned = weighted_ref[...].T
    for (shift, first), out_ref in zip(parts, out_refs):
        count = out_ref.shape[0]
        start = lax.rem(lax.axis_index("phi") + shift, 4) * (legendre_ref.shape[0] // 4) + first
        rows = legendre_ref[pl.ds(pl.multiple_of(start, 16), count), :]
        out_ref[...] = jnp.dot(rows, turned, preferred_element_type=f32).astype(out_ref.dtype)


def final_kernel(
    own_ref, a_ref, b_ref, radial_ref, linear_ref, gain_ref, *refs, first
):
    out_hbm, out_ref, sem = refs[-3:]
    block = pl.ds(first, a_ref.shape[0])
    total = own_ref[block, :] + a_ref[...].astype(f32) + b_ref[...].astype(f32)
    moved = jnp.dot(total.astype(bf16), radial_ref[...], preferred_element_type=f32)
    out_ref[...] = (linear_ref[block, :] + gain_ref[block, :] * moved).astype(bf16)
    departure = pltpu.make_async_copy(out_ref, out_hbm.at[block], sem)
    departure.start()
    departure.wait()


def local_call(kernel, name, outs, table, *args, scratch=(), limit=16, far=(), far_out=False, alias=None):
    vmem = pl.BlockSpec(memory_space=pltpu.VMEM)
    smem = pl.BlockSpec(memory_space=pltpu.SMEM)
    hbm = pl.BlockSpec(memory_space=pl.ANY)
    first = [] if table is None else [table]
    shapes = [jax.ShapeDtypeStruct(shape, dtype) for shape, dtype in outs]
    return pl.pallas_call(
        kernel,
        out_shape=shapes,
        in_specs=[smem] * len(first) + [hbm if n in far else vmem for n in range(len(args))],
        out_specs=[hbm if far_out else vmem] * len(shapes),
        scratch_shapes=scratch,
        input_output_aliases={} if alias is None else {alias: 0},
        compiler_params=pltpu.CompilerParams(vmem_limit_bytes=limit * 2**20),
        name=name,
    )(*first, *args)


def on_device(spectrum, legendre, orders, quadrature, radius, radial):
    degree_dev, _, columns = spectrum.shape
    ring = lax.axis_size("phi")
    group = lax.axis_size("lm")
    half = degree_dev // 2
    right = [(i, (i + 1) % ring) for i in range(ring)]
    left = [(i, (i - 1) % ring) for i in range(ring)]

    def go(x, way):
        return lax.ppermute(x, "phi", way)

    base = spectrum.reshape(degree_dev, columns)
    table = legendre.reshape(legendre.shape[0], legendre.shape[2])
    rows = table.shape[1]
    below = go(base, right)
    above = go(base, left)
    prepared = local_call(
        prepare_kernel, "prepare",
        [
            ((NPHI, 2 * group), bf16), ((2 * group, NPHI), bf16), ((columns, columns), bf16),
            ((degree_dev, columns), f32), ((degree_dev, columns), f32),
        ],
        orders, orders.reshape(1, group), base, radius.reshape(1, -1), radial,
        scratch=[
            pltpu.VMEM(base.shape, bf16), pltpu.VMEM(radial.shape, f32),
            pltpu.VMEM((columns, columns), bf16), pltpu.SemaphoreType.DMA((2,)),
        ],
        limit=60, far=(1, 3),
    )
    below, *prepared = lax.optimization_barrier((below, *prepared))
    synth, plain, straight, linear, gain = prepared
    far_top = go(below[:half], right)
    far_bottom = go(above[half:], left)
    (near,) = local_call(
        near_kernel, "near", [((columns, rows), f32)], orders, table, base, below, above
    )
    (latitude,) = local_call(
        far_kernel, "far", [((columns, rows), bf16)], orders, table, far_top, far_bottom, near,
    )

    def swap(x):
        x = x.reshape(group, columns // group, rows)
        x = lax.all_to_all(x, "lm", split_axis=0, concat_axis=0, tiled=True)
        return x.reshape(columns, rows)

    weighted = swap(
        grid_call(swap(latitude), synth, plain, quadrature, columns // group // 2, group)
    )

    def project(*parts):
        return local_call(
            functools.partial(project_kernel, parts=[part[:2] for part in parts]),
            "project", [((part[2], columns), part[3]) for part in parts], None, table, weighted,
        )

    less = half - SHIFT
    more = half + SHIFT
    far_top, far_bottom = project((2, 0, less, bf16), (2, less, more, bf16))
    from_left = go(far_top, right)
    from_right = go(far_bottom, left)
    above_bottom, below_top, above_top, below_bottom, own = project(
        (1, less, more, bf16), (3, 0, less, bf16), (1, 0, less, f32), (3, less, more, f32),
        (0, 0, degree_dev, f32),
    )
    sum_bottom = go(above_bottom, right)
    sum_top_left = go(below_top, left)
    sum_top = go((above_top + from_left.astype(f32)).astype(bf16), right)
    sum_bottom_left = go((below_bottom + from_right.astype(f32)).astype(bf16), left)
    def finish(first, one, two, *held):
        return local_call(
            functools.partial(final_kernel, first=first), "final",
            [((degree_dev, columns), bf16)], None, own, one, two, straight, linear, gain, *held,
            scratch=[pltpu.VMEM(one.shape, bf16), pltpu.SemaphoreType.DMA(())],
            far=(6,), far_out=True, alias=6 if held else None,
        )

    (result,) = finish(less, sum_bottom, sum_bottom_left)
    (result,) = finish(0, sum_top, sum_top_left, result)
    return result.reshape(degree_dev, 1, columns)


def solution(mesh):
    return jax.shard_map(
        on_device,
        mesh=mesh,
        in_specs=(P("phi", "lm", None), P(None, "lm", "phi"), P(), P("phi"), P(), P()),
        out_specs=P("phi", "lm", None),
        check_vma=False,
    )
```

```python
import functools
import math

import jax
import jax.numpy as jnp
from jax import lax
from jax.experimental import pallas as pl
from jax.experimental.pallas import tpu as pltpu
from jax.sharding import PartitionSpec as P

LMAX = 1023
NPHI = 3072
LANES = 128
BLOCK = 256
SHIFT = -16

time_step = 0.5
rotation = 2.0

bf16 = jnp.bfloat16
f32 = jnp.float32


def iota(shape, axis):
    return lax.broadcasted_iota(jnp.int32, shape, axis)


def permutation():
    row, column = iota((BLOCK, BLOCK), 0), iota((BLOCK, BLOCK), 1)
    perm = column == (row & 15) * 16 + 2 * (row >> 5) + ((row >> 4) & 1)
    back = row == (column & 15) * 16 + 2 * (column >> 5) + ((column >> 4) & 1)
    return as_ones(perm), as_ones(back)


def as_ones(mask):
    return jnp.where(mask, 1.0, 0.0).astype(bf16)


def grid_kernel(
    x_ref, synth_hbm, plain_hbm, quad_ref, y_ref,
    synth_ref, plain_ref, a_ref, product_ref, sems, *, step, orders
):
    arrivals = [
        pltpu.make_async_copy(src, dst, sems.at[n])
        for n, (src, dst) in enumerate([(synth_hbm, synth_ref), (plain_hbm, plain_ref)])
    ]
    for arrival in arrivals:
        arrival.start()
    blocks = x_ref.shape[0] // BLOCK
    rows = x_ref.shape[1]
    tiles = [(s, t) for s in range(a_ref.shape[0] // (rows // LANES)) for t in range(rows // LANES)]
    fields = 2 * len(tiles) // (rows // LANES)
    width = BLOCK // fields
    perm, back = permutation()
    quads = quad_ref[...].reshape(1, rows)
    turned = [
        jnp.dot(perm, x_ref[pl.ds(BLOCK * b, BLOCK), :], preferred_element_type=f32).astype(bf16)
        for b in range(blocks)
    ]
    for j, (s, t) in enumerate(tiles):
        for f in range(2):
            first = width * (2 * s + f)
            for b in range(blocks):
                a_ref[j, pl.ds(width * b, width), pl.ds(LANES * f, LANES)] = turned[b][
                    first : first + width, LANES * t : LANES * (t + 1)
                ]
    for arrival in arrivals:
        arrival.wait()
    scale = f32(math.sqrt(orders) / NPHI)
    signed = jnp.where(iota((LANES, 1), 0) & 16 == 0, scale, -scale)
    done = []
    for j, (s, t) in enumerate(tiles):
        slot = j % 2
        for n in range(NPHI // step):
            points = pl.ds(step * n, step)
            grid = jnp.dot(synth_ref[points, :], a_ref[j], preferred_element_type=f32)
            pol, tor = grid[:, :LANES], grid[:, LANES:]
            product_ref[slot, points, pl.ds(0, LANES)] = (pol * tor).astype(bf16)
            product_ref[slot, points, pl.ds(LANES, LANES)] = (pol * pol - tor * tor).astype(bf16)
        part = jnp.dot(plain_ref[...], product_ref[slot], preferred_element_type=f32)
        spectral = (part * signed).astype(bf16).astype(f32)
        quad = quads[:, LANES * t : LANES * (t + 1)]
        done.append((spectral * jnp.concatenate([quad, quad], 1)).astype(bf16))
    for b in range(blocks):
        strips = []
        for t in range(rows // LANES):
            strips.append(
                jnp.concatenate(
                    [
                        done[j][width * b : width * (b + 1), LANES * f : LANES * (f + 1)]
                        for j, (s, at) in enumerate(tiles) if at == t
                        for f in range(2)
                    ],
                    0,
                )
            )
        block = pl.ds(BLOCK * b, BLOCK)
        part = jnp.concatenate(strips, 1)
        y_ref[block, :] = jnp.dot(back, part, preferred_element_type=f32).astype(bf16)


def grid_call(x, synth, plain, quad, fields, orders):
    rows = x.shape[1]
    anywhere = pl.BlockSpec(memory_space=pltpu.HBM)
    vmem = pl.BlockSpec(memory_space=pltpu.VMEM)
    return pl.pallas_call(
        functools.partial(grid_kernel, step=512, orders=orders),
        out_shape=jax.ShapeDtypeStruct(x.shape, bf16),
        in_specs=[vmem, anywhere, anywhere, vmem],
        out_specs=vmem,
        scratch_shapes=[
            pltpu.VMEM(synth.shape, bf16),
            pltpu.VMEM(plain.shape, bf16),
            pltpu.VMEM((fields // 2 * rows // LANES, LANES, 2 * LANES), bf16),
            pltpu.VMEM((2, NPHI, 2 * LANES), bf16),
            pltpu.SemaphoreType.DMA((2,)),
        ],
        compiler_params=pltpu.CompilerParams(vmem_limit_bytes=24 * 2**20),
        name="grid",
    )(x, synth, plain, quad)


def wave(order, point, turn):
    product = order * point
    quarter = jnp.floor(product * f32(4.0 / NPHI) + f32(0.5))
    angle = (product - quarter * f32(NPHI / 4)) * f32(2.0 * math.pi / NPHI)
    square = angle * angle
    sine = angle * (1.0 + square * (-1 / 6 + square * (1 / 120 + square * (-1 / 5040))))
    cosine = 1.0 + square * (-0.5 + square * (1 / 24 + square * (-1 / 720 + square * (1 / 40320))))
    turns = quarter.astype(jnp.int32) + turn
    value = jnp.where(turns & 1 == 1, cosine, sine)
    return jnp.where(turns & 2 == 2, -value, value)


def trig_tables(orders, synth_ref, plain_ref, step=512):
    total = orders.shape[1]
    values = orders.astype(f32)
    picked = iota((2 * total, total), 0)
    picked = (picked >> 5) * 16 + (picked & 15) == iota((2 * total, total), 1)
    down = jnp.sum(jnp.where(picked, values, 0.0), axis=1, keepdims=True)
    diagonal = iota((total, total), 0) == iota((total, total), 1)
    column = jnp.sum(jnp.where(diagonal, values, 0.0), axis=1, keepdims=True)
    picked = iota((total, 2 * total), 1)
    picked = (picked >> 5) * 16 + (picked & 15) == iota((total, 2 * total), 0)
    across = jnp.sum(jnp.where(picked, column, 0.0), axis=0, keepdims=True)
    part = (iota((2 * total, 1), 0) >> 4) & 1
    part_across = (iota((1, 2 * total), 1) >> 4) & 1
    weight = jnp.where(across == 0, 1.0, 2.0) / f32(math.sqrt(total))
    weight = jnp.where(part_across == 0, weight, -weight)

    def body(i, carry):
        start = pl.multiple_of(i * step, step)
        point = (start + iota((step, 1), 0)).astype(f32)
        value = wave(across, point, 1 - part_across) * weight
        synth_ref[pl.ds(start, step), :] = value.astype(bf16)
        point = (start + iota((1, step), 1)).astype(f32)
        plain_ref[:, pl.ds(start, step)] = wave(down, point, 1 - part).astype(bf16)
        return carry

    lax.fori_loop(0, NPHI // step, body, 0)


def prepare_kernel(
    orders_ref, row_ref, base_hbm, radius_ref, radial_hbm,
    synth_ref, plain_ref, straight_ref, linear_ref, gain_ref,
    base_ref, radial_ref, low_ref, sems
):
    arrivals = [
        pltpu.make_async_copy(base_hbm, base_ref, sems.at[0]),
        pltpu.make_async_copy(radial_hbm, radial_ref, sems.at[1]),
    ]
    for arrival in arrivals:
        arrival.start()
    trig_tables(row_ref[...], synth_ref, plain_ref)
    for arrival in arrivals:
        arrival.wait()
    degrees, columns = base_ref.shape
    shells = columns // 4
    shell, column = iota((shells, columns), 0), iota((shells, columns), 1)
    home = column >> 2 == shell
    spread = [as_ones(home & ((column >> 1) & 1 == f)) for f in range(2)]
    row, column = iota((4 * LANES, columns), 0), iota((4 * LANES, columns), 1)
    same = row & 3 == column & 3
    grow = as_ones(iota((4 * LANES, LANES), 0) >> 2 == iota((4 * LANES, LANES), 1))
    high = radial_ref[...].astype(bf16)
    low = (radial_ref[...] - high.astype(f32)).astype(bf16)
    for term, out_ref in ((high, straight_ref), (low, low_ref)):
        wide = over_degrees(term[0], spread[0]) + over_degrees(term[1], spread[1])
        wide = wide.astype(bf16)
        for q in range(shells // LANES):
            tall = jnp.dot(grow, wide[LANES * q : LANES * (q + 1)], preferred_element_type=f32)
            out_ref[pl.ds(4 * LANES * q, 4 * LANES), :] = jnp.where(same, tall, 0.0).astype(bf16)
    radius = radius_ref[...]
    square = jnp.dot(
        radius * radius, jnp.where(home, 1.0, 0.0), precision=lax.Precision.HIGHEST,
        preferred_element_type=f32,
    )
    order = orders_ref[lax.axis_index("lm")]
    local = lax.axis_index("phi") * degrees + iota((degrees, 1), 0)
    degree = local.astype(f32)
    viscosity = 1.0 / (LMAX * (LMAX + 1.0))
    damping = 1.0 / (1.0 + time_step * viscosity * degree * (degree + 1.0) / square)
    damping = jnp.where(local >= order, damping, 0.0)
    gain_ref[...] = time_step * damping
    factor = time_step * rotation * order.astype(f32) / (degree + 1.0)
    row, column = iota((BLOCK, BLOCK), 0), iota((BLOCK, BLOCK), 1)
    turn = jnp.where(row == column ^ 3, jnp.where(column & 1 == 0, -1.0, 1.0), 0.0).astype(bf16)
    spin = [
        jnp.dot(base_ref[:, BLOCK * q : BLOCK * (q + 1)], turn, preferred_element_type=f32)
        for q in range(columns // BLOCK)
    ]
    stepped = base_ref[...].astype(f32) + factor * jnp.concatenate(spin, 1)
    high = stepped.astype(bf16)
    low = (stepped - high.astype(f32)).astype(bf16)
    linear = jnp.dot(high, straight_ref[...], preferred_element_type=f32)
    linear = linear + jnp.dot(low, straight_ref[...], preferred_element_type=f32)
    linear = linear + jnp.dot(high, low_ref[...], preferred_element_type=f32)
    linear_ref[...] = linear * damping


def masked_rows(orders_ref, legendre_ref, shift, first, count):
    start = lax.rem(lax.axis_index("phi") + shift, 4) * (legendre_ref.shape[0] // 4) + first
    rows = legendre_ref[pl.ds(pl.multiple_of(start, 128), count), :]
    degree = start + lax.broadcasted_iota(jnp.int32, rows.shape, 0)
    order = orders_ref[lax.axis_index("lm")]
    return jnp.where(degree >= order, rows.astype(f32), 0.0).astype(bf16)


def over_degrees(piece, rows):
    return lax.dot_general(piece, rows, (((0,), (0,)), ((), ())), preferred_element_type=f32)


def near_kernel(orders_ref, legendre_ref, base_ref, below_ref, above_ref, out_ref):
    rows = functools.partial(masked_rows, orders_ref, legendre_ref)
    count = base_ref.shape[0]
    total = over_degrees(base_ref[...], rows(0, 0, count))
    total = total + over_degrees(below_ref[...], rows(3, 0, count))
    out_ref[...] = total + over_degrees(above_ref[...], rows(1, 0, count))


def far_kernel(orders_ref, legendre_ref, top_ref, bottom_ref, near_ref, out_ref):
    half = top_ref.shape[0]
    rows = masked_rows(orders_ref, legendre_ref, 2, 0, 2 * half)
    for n in range(out_ref.shape[0] // BLOCK):
        block = pl.ds(BLOCK * n, BLOCK)
        piece = jnp.concatenate([top_ref[:, block], bottom_ref[:, block]], 0)
        out_ref[block, :] = (near_ref[block, :] + over_degrees(piece, rows)).astype(bf16)


def project_kernel(legendre_ref, weighted_ref, *out_refs, parts):
    turned = weighted_ref[...].T
    for (shift, first), out_ref in zip(parts, out_refs):
        count = out_ref.shape[0]
        start = lax.rem(lax.axis_index("phi") + shift, 4) * (legendre_ref.shape[0] // 4) + first
        rows = legendre_ref[pl.ds(pl.multiple_of(start, 16), count), :]
        out_ref[...] = jnp.dot(rows, turned, preferred_element_type=f32).astype(out_ref.dtype)


def final_kernel(
    own_ref, a_ref, b_ref, radial_ref, linear_ref, gain_ref, *refs, first
):
    out_hbm, out_ref, sem = refs[-3:]
    block = pl.ds(first, a_ref.shape[0])
    total = own_ref[block, :] + a_ref[...].astype(f32) + b_ref[...].astype(f32)
    moved = jnp.dot(total.astype(bf16), radial_ref[...], preferred_element_type=f32)
    out_ref[...] = (linear_ref[block, :] + gain_ref[block, :] * moved).astype(bf16)
    departure = pltpu.make_async_copy(out_ref, out_hbm.at[block], sem)
    departure.start()
    departure.wait()


def local_call(kernel, name, outs, table, *args, scratch=(), limit=16, far=(), far_out=False, alias=None):
    vmem = pl.BlockSpec(memory_space=pltpu.VMEM)
    smem = pl.BlockSpec(memory_space=pltpu.SMEM)
    hbm = pl.BlockSpec(memory_space=pl.ANY)
    first = [] if table is None else [table]
    shapes = [jax.ShapeDtypeStruct(shape, dtype) for shape, dtype in outs]
    return pl.pallas_call(
        kernel,
        out_shape=shapes,
        in_specs=[smem] * len(first) + [hbm if n in far else vmem for n in range(len(args))],
        out_specs=[hbm if far_out else vmem] * len(shapes),
        scratch_shapes=scratch,
        input_output_aliases={} if alias is None else {alias: 0},
        compiler_params=pltpu.CompilerParams(vmem_limit_bytes=limit * 2**20),
        name=name,
    )(*first, *args)


def on_device(spectrum, legendre, orders, quadrature, radius, radial):
    degree_dev, _, columns = spectrum.shape
    ring = lax.axis_size("phi")
    group = lax.axis_size("lm")
    half = degree_dev // 2
    right = [(i, (i + 1) % ring) for i in range(ring)]
    left = [(i, (i - 1) % ring) for i in range(ring)]

    def go(x, way):
        return lax.ppermute(x, "phi", way)

    base = spectrum.reshape(degree_dev, columns)
    table = legendre.reshape(legendre.shape[0], legendre.shape[2])
    rows = table.shape[1]
    below = go(base, right)
    above = go(base, left)
    prepared = local_call(
        prepare_kernel, "prepare",
        [
            ((NPHI, 2 * group), bf16), ((2 * group, NPHI), bf16), ((columns, columns), bf16),
            ((degree_dev, columns), f32), ((degree_dev, columns), f32),
        ],
        orders, orders.reshape(1, group), base, radius.reshape(1, -1), radial,
        scratch=[
            pltpu.VMEM(base.shape, bf16), pltpu.VMEM(radial.shape, f32),
            pltpu.VMEM((columns, columns), bf16), pltpu.SemaphoreType.DMA((2,)),
        ],
        limit=60, far=(1, 3),
    )
    below, *prepared = lax.optimization_barrier((below, *prepared))
    synth, plain, straight, linear, gain = prepared
    far_top = go(below[:half], right)
    far_bottom = go(above[half:], left)
    (near,) = local_call(
        near_kernel, "near", [((columns, rows), f32)], orders, table, base, below, above
    )
    (latitude,) = local_call(
        far_kernel, "far", [((columns, rows), bf16)], orders, table, far_top, far_bottom, near,
    )

    def swap(x):
        x = x.reshape(group, columns // group, rows)
        x = lax.all_to_all(x, "lm", split_axis=0, concat_axis=0, tiled=True)
        return x.reshape(columns, rows)

    weighted = swap(
        grid_call(swap(latitude), synth, plain, quadrature, columns // group // 2, group)
    )

    def project(*parts):
        return local_call(
            functools.partial(project_kernel, parts=[part[:2] for part in parts]),
            "project", [((part[2], columns), part[3]) for part in parts], None, table, weighted,
        )

    less = half - SHIFT
    more = half + SHIFT
    far_top, far_bottom = project((2, 0, less, bf16), (2, less, more, bf16))
    from_left = go(far_top, right)
    from_right = go(far_bottom, left)
    above_bottom, below_top, above_top, below_bottom, own = project(
        (1, less, more, bf16), (3, 0, less, bf16), (1, 0, less, f32), (3, less, more, f32),
        (0, 0, degree_dev, f32),
    )
    sum_bottom = go(above_bottom, right)
    sum_top_left = go(below_top, left)
    sum_top = go((above_top + from_left.astype(f32)).astype(bf16), right)
    sum_bottom_left = go((below_bottom + from_right.astype(f32)).astype(bf16), left)
    def finish(first, one, two, *held):
        return local_call(
            functools.partial(final_kernel, first=first), "final",
            [((degree_dev, columns), bf16)], None, own, one, two, straight, linear, gain, *held,
            scratch=[pltpu.VMEM(one.shape, bf16), pltpu.SemaphoreType.DMA(())],
            far=(6,), far_out=True, alias=6 if held else None,
        )

    (result,) = finish(less, sum_bottom, sum_bottom_left)
    (result,) = finish(0, sum_top, sum_top_left, result)
    return result.reshape(degree_dev, 1, columns)


def solution(mesh):
    return jax.shard_map(
        on_device,
        mesh=mesh,
        in_specs=(P("phi", "lm", None), P(None, "lm", "phi"), P(), P("phi"), P(), P()),
        out_specs=P("phi", "lm", None),
        check_vma=False,
    )
```
